256 devices in a mesh: ctx: 64 (over x, z, core), head: 4 (over y).
Axes of the slice: x: 4, y: 4, z: 8, core: 2. Of those that a mesh axis runs over, the one named last changes fastest.
Arguments:
- queries: bfloat16 [16384, 4096], P('ctx', 'head'), may hold values from -6 to 6
- key_rows: bfloat16 [16384, 4096], P('ctx', 'head'), may hold values from -3 to 3
- value_rows: bfloat16 [16384, 4096], P('ctx', 'head'), may hold values from -12 to 12
- gate_logits: bfloat16 [16384, 4096], P('ctx', 'head'), may hold values from -6 to 6
- norm_gain: float32 [4096], P('head'), may hold values from 0.5 to 1.5
- log_decay: float32 [16384, 32], P('ctx', 'head')
- cotangent: bfloat16 [16384, 4096], P('ctx', 'head'), may hold values from -6 to 6
Outputs:
- attended: bfloat16 [16384, 4096], P('ctx', 'head')
- grad_queries: bfloat16 [16384, 4096], P('ctx', 'head')
- grad_keys: bfloat16 [16384, 4096], P('ctx', 'head')
- grad_values: bfloat16 [16384, 4096], P('ctx', 'head')
- grad_gate: bfloat16 [16384, 4096], P('ctx', 'head')
- grad_decay: float32 [16384, 32], P('ctx', 'head')
- grad_gain: float32 [4096], P('head')
The draws below stay inside these ranges and needn't reach their ends.
All inputs are finite; a program needn't handle non-finite values.
Results may differ from the reference program's by a relative error of at most 0.0069.
Values may be sent and summed in bfloat16 or wider, within the bound.
No kernel may reach another device: no remote copies, remote signals or barrier semaphores. Data moves between devices by JAX's collectives and lax.ppermute only.
A program may use at most 192 MiB of HBM per device.

```python
import math
import jax
import jax.numpy as jnp
from jax import lax

HEAD_COUNT = 32
HD = 128
TOK_DEV = 256
TOKEN_COUNT = 16384
N_CTX = 64


def draw_queries(key, part):
    key_base = jax.random.fold_in(key, 11)
    key_noise, key_scale = jax.random.split(key_base)
    row_scale = jnp.exp(jax.random.uniform(key_scale, (TOKEN_COUNT, 1), jnp.float32, math.log(0.3), math.log(3.0)))
    noise = jnp.clip(jax.random.normal(key_noise, (TOKEN_COUNT, HEAD_COUNT * HD), jnp.float32), -4.0, 4.0)
    return (0.5 * noise * row_scale).astype(jnp.bfloat16)


def draw_value_rows(key, part):
    key_base = jax.random.fold_in(key, 23)
    key_noise, key_scale = jax.random.split(key_base, 2)
    column_scale = jnp.exp(jax.random.uniform(key_scale, (1, HEAD_COUNT * HD), jnp.float32, math.log(0.3), math.log(3.0)))
    noise = jnp.clip(jax.random.normal(key_noise, (TOKEN_COUNT, HEAD_COUNT * HD), jnp.float32), -4.0, 4.0)
    return (noise * column_scale).astype(jnp.bfloat16)


def draw_log_decay(key, part):
    key_base = jax.random.fold_in(key, 37)
    key_kind, key_fast, key_slow, key_token, key_block, location_random_key, loss_random_key = jax.random.split(key_base, 7)
    fast_head = jax.random.randint(key_kind, (HEAD_COUNT,), 0, 2) == 1
    fast_rate = 1.0 / jax.random.uniform(key_fast, (HEAD_COUNT,), jnp.float32, 30.0, 400.0)
    slow_rate = jax.random.uniform(key_slow, (HEAD_COUNT,), jnp.float32, 0.05, 0.25) * math.log(10.0) / TOKEN_COUNT
    starting_rate = jnp.where(fast_head, fast_rate, slow_rate)
    token_multiplier = jnp.exp(jax.random.uniform(key_token, (TOKEN_COUNT, HEAD_COUNT), jnp.float32, math.log(0.5), math.log(2.0)))
    block_multiplier = jnp.exp(jax.random.uniform(key_block, (TOKEN_COUNT // TOK_DEV, 1, HEAD_COUNT), jnp.float32, math.log(0.5), math.log(2.0)))
    block_multiplier = jnp.broadcast_to(block_multiplier, (TOKEN_COUNT // TOK_DEV, TOK_DEV, HEAD_COUNT)).reshape(TOKEN_COUNT, HEAD_COUNT)
    spike_location = jax.random.randint(location_random_key, (3, 1, HEAD_COUNT), 0, TOKEN_COUNT)
    spike_loss_term = jax.random.uniform(loss_random_key, (3, 1, HEAD_COUNT), jnp.float32, math.log(0.6), math.log(0.8))
    token_positions = jnp.arange(TOKEN_COUNT)[None, :, None]
    spike_events = jnp.sum(jnp.where(token_positions == spike_location, spike_loss_term, 0.0), axis=0)
    return -starting_rate[None, :] * token_multiplier * block_multiplier + spike_events


def shard_levels(rng, extent, cuts, low, high):
    level, own = 1.0, jax.random.fold_in(rng, 6)
    for dim, blocks in cuts:
        draws = jnp.exp(jax.random.uniform(jax.random.fold_in(own, dim), (blocks,), jnp.float32, low / len(cuts), high / len(cuts)))
        level = level * jnp.repeat(draws, extent[dim] // blocks).reshape([-1 if axis == dim else 1 for axis in range(len(extent))])
    return level


def normal_values(rng, extent, deviation, reach, shards=(), kind=jnp.bfloat16):
    gain = shard_levels(rng, extent, shards, -0.22, 0.18) if shards else 1.0
    result = jax.random.normal(rng, extent, jnp.float32) * deviation * gain
    return jnp.minimum(jnp.maximum(result, -reach), reach).astype(kind)


def setup_inputs(seed: int = 0) -> dict:
    key_of = jax.random.split(jax.random.key(seed), 8)
    return {
        "queries": draw_queries(jax.random.fold_in(key_of[7], 71), 0),
        "key_rows": normal_values(key_of[1], (TOKEN_COUNT, HEAD_COUNT * HD), 0.5, 3.0, ((0, 64), (1, 4))),
        "value_rows": draw_value_rows(jax.random.fold_in(key_of[7], 71), 0),
        "gate_logits": normal_values(key_of[3], (TOKEN_COUNT, HEAD_COUNT * HD), 1.0, 6.0, ((0, 64), (1, 4))),
        "norm_gain": jnp.clip(1.0 + 0.1 * jax.random.normal(key_of[4], (HEAD_COUNT * HD,), jnp.float32), 0.5, 1.5),
        "log_decay": draw_log_decay(jax.random.fold_in(key_of[7], 71), 0),
        "cotangent": normal_values(key_of[6], (TOKEN_COUNT, HEAD_COUNT * HD), 1.0, 6.0, ((0, 64), (1, 4))),
    }


EPSILON = 1e-05

def rounded(values):
    return lax.optimization_barrier(values.astype(jnp.bfloat16)).astype(jnp.float32)

def block_parts(query_block, key_block, value_block, decay_block):
    query_f = query_block.astype(jnp.float32)
    key_f = key_block.astype(jnp.float32)
    value_f = value_block.astype(jnp.float32)
    cumulative = jnp.cumsum(decay_block, axis=0)
    last_log = cumulative[-1]
    length = decay_block.shape[0]
    causal = (jnp.arange(length)[None, :] <= jnp.arange(length)[:, None])[None]
    log_gap = cumulative.T[:, :, None] - cumulative.T[:, None, :]
    decay_mask = jnp.where(causal, jnp.exp(jnp.where(causal, log_gap, 0.0)), 0.0)
    scores = jnp.einsum('ihd,jhd->hij', query_f, key_f)
    weights = rounded(decay_mask * scores)
    intra_sum = jnp.einsum('hij,jhe->ihe', weights, value_f)
    query_decayed = rounded(query_f * jnp.exp(cumulative)[:, :, None])
    key_fade = jnp.exp(last_log[None, :] - cumulative)
    key_decayed = rounded(key_f * key_fade[:, :, None])
    local_state = rounded(jnp.einsum('jhd,jhe->hde', key_decayed, value_f))
    block_decay = jnp.exp(last_log)
    return (query_f, key_f, value_f, cumulative, decay_mask, scores, weights, intra_sum, query_decayed, key_fade, local_state, block_decay)

def reference(queries, key_rows, value_rows, gate_logits, norm_gain, log_decay, cotangent):
    shape_four = (N_CTX, TOK_DEV, HEAD_COUNT, HD)
    query_blocks = queries.reshape(shape_four)
    key_blocks = key_rows.reshape(shape_four)
    value_blocks = value_rows.reshape(shape_four)
    decay_blocks = log_decay.reshape(N_CTX, TOK_DEV, HEAD_COUNT)
    zero_state = jnp.zeros((HEAD_COUNT, HD, HD), jnp.float32)

    def forward(prior_state, blocks):
        parts = block_parts(*blocks)
        intra_sum, query_decayed, local_state, block_decay = (parts[7], parts[8], parts[10], parts[11])
        inter_sum = jnp.einsum('ihd,hde->ihe', query_decayed, rounded(prior_state))
        following = block_decay[:, None, None] * prior_state + local_state
        return (following, (intra_sum + inter_sum, prior_state))
    _, (attn_blocks, prior_states) = lax.scan(forward, zero_state, (query_blocks, key_blocks, value_blocks, decay_blocks))
    full_width = HEAD_COUNT * HD
    attention = attn_blocks.reshape(TOKEN_COUNT, full_width)
    gate_open = jax.nn.sigmoid(gate_logits.astype(jnp.float32))
    upstream = cotangent.astype(jnp.float32)
    gain_row = norm_gain[None, :]
    root_mean = jnp.sqrt(lax.optimization_barrier(jnp.sum(attention * attention, axis=1)) / full_width + EPSILON)
    normalized = attention / root_mean[:, None]
    scaled = normalized * gain_row
    attended = (scaled * gate_open).astype(jnp.bfloat16)
    grad_gate = (upstream * scaled * gate_open * (1.0 - gate_open)).astype(jnp.bfloat16)
    through_gate = upstream * gate_open
    grad_gain = lax.optimization_barrier(jnp.sum(through_gate * normalized, axis=0))
    cross_dot = lax.optimization_barrier(jnp.sum(through_gate * gain_row * normalized, axis=1))
    grad_attention = rounded((through_gate * gain_row - normalized * (cross_dot / full_width)[:, None]) / root_mean[:, None])
    grad_blocks = grad_attention.reshape(shape_four)

    def backward(later_state, blocks):
        query_block, key_block, value_block, decay_block, prior_state, grad_block = blocks
        parts = block_parts(query_block, key_block, value_block, decay_block)
        query_f, key_f, value_f, cumulative, decay_mask, scores, weights, intra_sum, query_decayed, key_fade, local_state, block_decay = parts
        prior_bf = rounded(prior_state)
        later_bf = rounded(later_state)
        inter_sum = jnp.einsum('ihd,hde->ihe', query_decayed, prior_bf)
        outgoing = jnp.einsum('ihd,ihe->hde', query_decayed, grad_block)
        grad_scores = jnp.einsum('ihe,jhe->hij', grad_block, value_f)
        products = decay_mask * scores * grad_scores
        mixed = rounded(decay_mask * grad_scores)
        grad_q = jnp.einsum('hij,jhd->ihd', mixed, key_f) + jnp.exp(cumulative)[:, :, None] * jnp.einsum('ihe,hde->ihd', grad_block, prior_bf)
        value_pull = jnp.einsum('jhe,hde->jhd', value_f, later_bf)
        key_pull = jnp.einsum('jhd,hde->jhe', key_f, later_bf)
        grad_k = jnp.einsum('hij,ihd->jhd', mixed, query_f) + key_fade[:, :, None] * value_pull
        grad_v = jnp.einsum('hij,ihe->jhe', weights, grad_block) + key_fade[:, :, None] * key_pull
        state_pull = key_fade * lax.optimization_barrier(jnp.sum(key_f * value_pull, axis=2))
        grad_cum = lax.optimization_barrier(jnp.sum(inter_sum * grad_block, axis=2)) + lax.optimization_barrier(jnp.sum(products, axis=2)).T - lax.optimization_barrier(jnp.sum(products, axis=1)).T - state_pull
        tail_term = lax.optimization_barrier(jnp.sum(state_pull, axis=0)) + block_decay * lax.optimization_barrier(jnp.sum(later_state * prior_state, axis=(1, 2)))
        is_last = (jnp.arange(TOK_DEV) == TOK_DEV - 1)[:, None]
        grad_cum = grad_cum + jnp.where(is_last, tail_term[None, :], 0.0)
        grad_dec = jnp.flip(jnp.cumsum(jnp.flip(grad_cum, 0), axis=0), 0)
        earlier_state = outgoing + block_decay[:, None, None] * later_state
        return (earlier_state, (grad_q.astype(jnp.bfloat16), grad_k.astype(jnp.bfloat16), grad_v.astype(jnp.bfloat16), grad_dec))
    _, (grad_q_blocks, grad_k_blocks, grad_v_blocks, grad_dec_blocks) = lax.scan(backward, zero_state, (query_blocks, key_blocks, value_blocks, decay_blocks, prior_states, grad_blocks), reverse=True)
    return (attended, grad_q_blocks.reshape(TOKEN_COUNT, full_width), grad_k_blocks.reshape(TOKEN_COUNT, full_width), grad_v_blocks.reshape(TOKEN_COUNT, full_width), grad_gate, grad_dec_blocks.reshape(TOKEN_COUNT, HEAD_COUNT), grad_gain)
```

```python
import functools

import jax
import jax.numpy as jnp
from jax import lax
from jax.experimental import pallas as pl
from jax.experimental.pallas import tpu as pltpu
from jax.sharding import PartitionSpec as P

EPSILON = 1e-05
HD = 128
ROWS = 16
EXTRA = 8
F32 = jnp.float32
BF16 = jnp.bfloat16
NEGATIVE = -1e30


def dot(a, b, contract=(1, 0)):
    dims = (((contract[0],), (contract[1],)), ((), ()))
    return lax.dot_general(a, b, dims, preferred_element_type=F32)


def three_parts(value):
    high = value.astype(BF16)
    rest = value - high.astype(F32)
    middle = rest.astype(BF16)
    low = (rest - middle.astype(F32)).astype(BF16)
    return high, middle, low


def triangle_bf(length, flipped=False):
    row = lax.broadcasted_iota(jnp.int32, (length, length), 0)
    col = lax.broadcasted_iota(jnp.int32, (length, length), 1)
    return jnp.where(row <= col if flipped else col <= row, 1.0, 0.0).astype(BF16)


def exact_sums(ones, value):
    return sum(dot(ones, part) for part in three_parts(value))


def small_rows(value):
    high, middle, low = (part.astype(F32) for part in three_parts(value))
    row = lax.broadcasted_iota(jnp.int32, (EXTRA, HD), 0)
    block = jnp.where(row == 0, high, jnp.where(row == 1, middle, jnp.where(row == 2, low, 0.0)))
    return block.astype(BF16)


def joined_rows(block):
    block = block.astype(F32)
    return block[0:1] + block[1:2] + block[2:3]


def masked_gap(cum_col, cum_row, low, high, left, right):
    gap = cum_col[low:high] - cum_row[:, left:right]
    if right <= low:
        return gap
    row = lax.broadcasted_iota(jnp.int32, gap.shape, 0) + low
    col = lax.broadcasted_iota(jnp.int32, gap.shape, 1) + left
    return jnp.where(col <= row, gap, NEGATIVE)


def decay_blocks(cum_col, cum_row):
    length = cum_col.shape[0]
    half = length // 2
    top = jnp.exp(masked_gap(cum_col, cum_row, 0, half, 0, half))
    bottom = jnp.exp(masked_gap(cum_col, cum_row, half, length, 0, length))
    return top, bottom


def local_state_kernel(heads, k_ref, v_ref, ld_ref, pay_ref, cum_ref, cumt_ref, loc_ref):
    length = k_ref.shape[0]
    cum = exact_sums(triangle_bf(length), ld_ref[...])
    cum_ref[...] = cum
    wide = jnp.concatenate([cum, jnp.zeros((length, HD - heads), F32)], axis=1)
    cumt_ref[...] = wide.T[:heads]
    last = cum[length - 1 : length]
    fade = jnp.exp(last - cum)
    for h in range(heads):
        cols = slice(h * HD, (h + 1) * HD)
        decayed = (k_ref[:, cols].astype(F32) * fade[:, h : h + 1]).astype(BF16)
        state = dot(decayed, v_ref[:, cols], (0, 0)).astype(BF16)
        loc_ref[h] = state
        rows = small_rows(jnp.broadcast_to(last[:, h : h + 1], (1, HD)))
        for part in range(HD // ROWS):
            pay_ref[h * (HD // ROWS) + part, :ROWS] = state[part * ROWS : (part + 1) * ROWS]
            pay_ref[h * (HD // ROWS) + part, ROWS:] = rows


def forward_scan_kernel(pay_ref, out_ref, decay_ref):
    state = jnp.zeros((ROWS, HD), F32)
    for c in range(pay_ref.shape[0]):
        out_ref[c] = state.astype(BF16)
        decay = jnp.exp(joined_rows(pay_ref[c, ROWS:]))
        decay_ref[c : c + 1] = decay
        state = decay * state + pay_ref[c, :ROWS].astype(F32)


def backward_scan_kernel(pay_ref, decay_ref, out_ref):
    state = jnp.zeros((ROWS, HD), F32)
    total = jnp.zeros((1, HD), F32)
    for c in reversed(range(pay_ref.shape[0])):
        out_ref[c, :ROWS] = state.astype(BF16)
        state = decay_ref[c : c + 1] * state + pay_ref[c, :ROWS].astype(F32)
        total = total + joined_rows(pay_ref[c, ROWS:])
    rows = small_rows(total)
    for c in range(pay_ref.shape[0]):
        out_ref[c, ROWS:] = rows


def attention_kernel(
    heads, q_ref, k_ref, v_ref, gate_ref, cot_ref, gain_ref, cum_ref, cumt_ref, prior_ref,
    attn_ref, weights_ref, sums_ref,
):
    length = q_ref.shape[0]
    half = length // 2
    squares = jnp.zeros((length, HD), F32)
    cross = jnp.zeros((length, HD), F32)
    cum = cum_ref[...]
    for h in range(heads):
        cols = slice(h * HD, (h + 1) * HD)
        q, k, v = q_ref[:, cols], k_ref[:, cols], v_ref[:, cols]
        top, bottom = decay_blocks(cum[:, h : h + 1], cumt_ref[h : h + 1])
        top = (top * dot(q[:half], k[:half], (1, 1))).astype(BF16)
        bottom = (bottom * dot(q[half:], k, (1, 1))).astype(BF16)
        weights_ref[h, :half, :half] = top
        weights_ref[h, :half, half:] = jnp.zeros((half, length - half), BF16)
        weights_ref[h, half:] = bottom
        decayed = (q.astype(F32) * jnp.exp(cum[:, h : h + 1])).astype(BF16)
        attn = dot(decayed, prior_ref[h]) + jnp.concatenate([dot(top, v[:half]), dot(bottom, v)])
        attn_ref[:, cols] = attn
        opened = jax.nn.sigmoid(gate_ref[:, cols].astype(F32))
        upstream = cot_ref[:, cols].astype(F32) * opened * gain_ref[:, cols]
        squares = squares + attn * attn
        cross = cross + upstream * attn
    sums_ref[...] = jnp.concatenate(
        [
            jnp.sum(squares.T, axis=0, keepdims=True),
            jnp.sum(cross.T, axis=0, keepdims=True),
            jnp.zeros((6, length), F32),
        ]
    )


def norm_kernel(
    heads, full_width, q_ref, gate_ref, cot_ref, gain_ref, cum_ref, attn_ref, *rest
):
    sums_refs, (attended_ref, ggate_ref, grad_ref, pay_ref) = rest[:-4], rest[-4:]
    length = q_ref.shape[0]
    sums = sum(ref[...] for ref in sums_refs)
    inverse_row = 1.0 / jnp.sqrt(sums[0:1] / full_width + EPSILON)
    cross_row = sums[1:2] * inverse_row / full_width
    inverse = jnp.broadcast_to(inverse_row, (HD, length)).T
    cross = jnp.broadcast_to(cross_row, (HD, length)).T
    cum = cum_ref[...]
    for h in range(heads):
        cols = slice(h * HD, (h + 1) * HD)
        opened = jax.nn.sigmoid(gate_ref[:, cols].astype(F32))
        through = cot_ref[:, cols].astype(F32) * opened
        gain = gain_ref[:, cols]
        normalized = attn_ref[:, cols] * inverse
        scaled = normalized * gain
        attended_ref[:, cols] = (scaled * opened).astype(BF16)
        ggate_ref[:, cols] = (through * scaled * (1.0 - opened)).astype(BF16)
        gain_sum = jnp.sum(through * normalized, axis=0, keepdims=True)
        grad = ((through * gain - normalized * cross) * inverse).astype(BF16)
        grad_ref[:, cols] = grad
        decayed = (q_ref[:, cols].astype(F32) * jnp.exp(cum[:, h : h + 1])).astype(BF16)
        outgoing = dot(decayed, grad, (0, 0)).astype(BF16)
        rows = small_rows(gain_sum)
        for part in range(HD // ROWS):
            pay_ref[h * (HD // ROWS) + part, :ROWS] = outgoing[part * ROWS : (part + 1) * ROWS]
            pay_ref[h * (HD // ROWS) + part, ROWS:] = rows


def gradient_kernel(
    heads, q_ref, k_ref, v_ref, cum_ref, cumt_ref, weights_ref, attn_ref, grad_ref, prior_ref,
    loc_ref, back_ref, gq_ref, gk_ref, gv_ref, gdecay_ref, ggain_ref,
):
    length = q_ref.shape[0]
    half = length // 2
    parts = HD // ROWS
    cum = cum_ref[...]
    last = cum[length - 1 : length]
    lane = lax.broadcasted_iota(jnp.int32, (1, HD), 1)
    tails = jnp.zeros((1, HD), F32)
    columns = []
    for h in range(heads):
        cols = slice(h * HD, (h + 1) * HD)
        q, k, v, grad = q_ref[:, cols], k_ref[:, cols], v_ref[:, cols], grad_ref[:, cols]
        prior = prior_ref[h]
        later = jnp.concatenate([back_ref[h * parts + part, :ROWS] for part in range(parts)])
        ggain_ref[:, cols] = joined_rows(back_ref[h * parts, ROWS:])
        top, bottom = decay_blocks(cum[:, h : h + 1], cumt_ref[h : h + 1])
        top = (top * dot(grad[:half], v[:half], (1, 1))).astype(BF16)
        bottom = (bottom * dot(grad[half:], v, (1, 1))).astype(BF16)
        gq = jnp.concatenate([dot(top, k[:half]), dot(bottom, k)])
        gq = gq + jnp.exp(cum[:, h : h + 1]) * dot(grad, prior, (1, 1))
        gq_ref[:, cols] = gq.astype(BF16)
        mixed = jnp.concatenate(
            [jnp.concatenate([top, jnp.zeros((half, length - half), BF16)], axis=1), bottom]
        )
        fade = jnp.exp(last[:, h : h + 1] - cum[:, h : h + 1])
        gk = dot(mixed, q, (0, 0)) + fade * dot(v, later, (1, 1))
        gk_ref[:, cols] = gk.astype(BF16)
        gv = dot(weights_ref[h], grad, (0, 0)) + fade * dot(k, later)
        gv_ref[:, cols] = gv.astype(BF16)
        following = loc_ref[h].astype(F32) + jnp.exp(last[:, h : h + 1]) * prior.astype(F32)
        tail = jnp.sum(following * later.astype(F32))
        tails = jnp.where(lane == h, tail, tails)
        change = attn_ref[:, cols] * grad.astype(F32) - k.astype(F32) * gk
        columns.append(jnp.sum(change, axis=1, keepdims=True))
    change = jnp.concatenate(columns, axis=1)
    gdecay_ref[...] = exact_sums(triangle_bf(length, True), change) + tails[:, :heads]


def local_call(kernel, outs, args, flops=0, moved=0):
    return pl.pallas_call(
        kernel,
        out_shape=[jax.ShapeDtypeStruct(shape, kind) for shape, kind in outs],
        compiler_params=pltpu.CompilerParams(vmem_limit_bytes=48 * 2**20),
    )(*args)


def exchange(payload):
    return lax.all_to_all(payload, "ctx", 0, 0, tiled=True)


def per_device(queries, key_rows, value_rows, gate_logits, norm_gain, log_decay, cotangent):
    length, width = queries.shape
    heads = log_decay.shape[1]
    count = lax.axis_size("ctx")
    full_width = width * lax.axis_size("head")
    gain = norm_gain.reshape(1, width)
    state = (heads, HD, HD)
    chunks = heads * HD // ROWS
    payload, cum, cumt, local = local_call(
        functools.partial(local_state_kernel, heads),
        [((chunks, ROWS + EXTRA, HD), BF16), ((length, heads), F32), ((heads, length), F32), (state, BF16)],
        (key_rows, value_rows, log_decay),
    )
    arrived = exchange(payload)
    scanned, decays = local_call(
        forward_scan_kernel, [((count, ROWS, HD), BF16), ((count, HD), F32)], (arrived,)
    )
    prior = exchange(scanned).reshape(state)
    attn, weights, sums = local_call(
        functools.partial(attention_kernel, heads),
        [((length, width), F32), ((heads, length, length), BF16), ((8, length), F32)],
        (queries, key_rows, value_rows, gate_logits, cotangent, gain, cum, cumt, prior),
    )
    size = lax.axis_size("head")
    others = [
        lax.ppermute(sums, "head", [(i, (i + step) % size) for i in range(size)])
        for step in range(1, size)
    ]
    attended, grad_gate, grad, payload = local_call(
        functools.partial(norm_kernel, heads, full_width),
        [((length, width), BF16)] * 3 + [((chunks, ROWS + EXTRA, HD), BF16)],
        (queries, gate_logits, cotangent, gain, cum, attn, sums, *others),
    )
    arrived = exchange(payload)
    (scanned,) = local_call(
        backward_scan_kernel, [((count, ROWS + EXTRA, HD), BF16)], (arrived, decays)
    )
    back = exchange(scanned)
    grad_q, grad_k, grad_v, grad_decay, grad_gain = local_call(
        functools.partial(gradient_kernel, heads),
        [((length, width), BF16)] * 3 + [((length, heads), F32), ((1, width), F32)],
        (queries, key_rows, value_rows, cum, cumt, weights, attn, grad, prior, local, back),
    )
    return attended, grad_q, grad_k, grad_v, grad_gate, grad_decay, grad_gain.reshape(width)


def solution(mesh):
    tokens = P("ctx", "head")
    return jax.shard_map(
        per_device,
        mesh=mesh,
        in_specs=(tokens, tokens, tokens, tokens, P("head"), tokens, tokens),
        out_specs=(tokens, tokens, tokens, tokens, tokens, tokens, P("head")),
        check_vma=False,
    )
```

```python
import functools

import jax
import jax.numpy as jnp
from jax import lax
from jax.experimental import pallas as pl
from jax.experimental.pallas import tpu as pltpu
from jax.sharding import Mesh
from jax.sharding import PartitionSpec as P

EPSILON = 1e-05
HD = 128
ROWS = 16
EXTRA = 8
F32 = jnp.float32
BF16 = jnp.bfloat16
NEGATIVE = -1e30
WORK = 500_000_000


def dot(a, b, contract=(1, 0)):
    dims = (((contract[0],), (contract[1],)), ((), ()))
    return lax.dot_general(a, b, dims, preferred_element_type=F32)


def three_parts(value):
    high = value.astype(BF16)
    rest = value - high.astype(F32)
    middle = rest.astype(BF16)
    low = (rest - middle.astype(F32)).astype(BF16)
    return high, middle, low


def triangle_bf(length, flipped=False):
    row = lax.broadcasted_iota(jnp.int32, (length, length), 0)
    col = lax.broadcasted_iota(jnp.int32, (length, length), 1)
    return jnp.where(row <= col if flipped else col <= row, 1.0, 0.0).astype(BF16)


def exact_sums(ones, value):
    return sum(dot(ones, part) for part in three_parts(value))


def small_rows(*values):
    row = lax.broadcasted_iota(jnp.int32, (EXTRA, HD), 0)
    block = jnp.zeros((EXTRA, HD), F32)
    for place, value in enumerate(values):
        for turn, part in enumerate(three_parts(value)):
            block = jnp.where(row == 3 * place + turn, part.astype(F32), block)
    return block.astype(BF16)


def joined_rows(block, place=0):
    block = block[...].astype(F32)
    at = 3 * place
    return block[at : at + 1] + block[at + 1 : at + 2] + block[at + 2 : at + 3]


def masked_gap(cum_col, cum_row, low, high, left, right):
    gap = cum_col[low:high] - cum_row[:, left:right]
    if right <= low:
        return gap
    row = lax.broadcasted_iota(jnp.int32, gap.shape, 0) + low
    col = lax.broadcasted_iota(jnp.int32, gap.shape, 1) + left
    return jnp.where(col <= row, gap, NEGATIVE)


def decay_blocks(cum_col, cum_row):
    length = cum_col.shape[0]
    half = length // 2
    top = jnp.exp(masked_gap(cum_col, cum_row, 0, half, 0, half))
    bottom = jnp.exp(masked_gap(cum_col, cum_row, half, length, 0, length))
    return top, bottom


def one_of(first, if_first, if_second):
    return jnp.where(first, if_first, if_second)


def local_state_kernel(heads, k_ref, v_ref, ldt_ref, loc_ref, theirs_ref, cum_ref, cumt_ref):
    length = k_ref.shape[0]
    half = heads // 2
    core = lax.axis_index("core")
    ones = triangle_bf(length, True)
    cumt = sum(dot(part, ones) for part in three_parts(ldt_ref[...]))
    cumt_ref[...] = cumt
    cum = jnp.concatenate([cumt, jnp.zeros((HD - heads, length), F32)]).T[:, :heads]
    cum_ref[...] = cum
    last = cum[length - 1 : length]
    fade = jnp.exp(last - cum)
    for h in range(heads):
        cols = slice(h * HD, (h + 1) * HD)
        decayed = (k_ref[:, cols].astype(F32) * fade[:, h : h + 1]).astype(BF16)
        loc_ref[h] = dot(decayed, v_ref[:, cols], (0, 0)).astype(BF16)
    theirs_ref[:, :HD] = loc_ref[pl.ds((1 - core) * half, half)]
    for h in range(half):
        value = one_of(core == 0, last[:, half + h : half + h + 1], last[:, h : h + 1])
        theirs_ref[h, HD:] = small_rows(jnp.broadcast_to(value, (1, HD)))


def pair_logs(core, half, h, cumt_ref, got_ref):
    length = cumt_ref.shape[1]
    own = one_of(
        core == 0, cumt_ref[h : h + 1, length - 1 :], cumt_ref[half + h : half + h + 1, length - 1 :]
    )
    own = jnp.broadcast_to(own, (1, HD))
    other = joined_rows(got_ref[h, HD:])
    return one_of(core == 0, own, other), one_of(core == 0, other, own)


def pair_values(core, half, h, loc_ref, got_ref):
    own = loc_ref[core * half + h].astype(F32)
    other = got_ref[h, :HD].astype(F32)
    return one_of(core == 0, own, other), one_of(core == 0, other, own)


def put_chunks(pay_ref, h, state, rows):
    parts = HD // ROWS
    for part in range(parts):
        pay_ref[h * parts + part, :ROWS] = state[part * ROWS : (part + 1) * ROWS]
        pay_ref[h * parts + part, ROWS:] = rows


def forward_join_kernel(half, loc_ref, got_ref, cumt_ref, pay_ref):
    core = lax.axis_index("core")
    for h in range(half):
        log0, log1 = pair_logs(core, half, h, cumt_ref, got_ref)
        state0, state1 = pair_values(core, half, h, loc_ref, got_ref)
        both = jnp.exp(log1) * state0 + state1
        put_chunks(pay_ref, h, both.astype(BF16), small_rows(log0 + log1))


def forward_scan_kernel(pay_ref, out_ref, decay_ref, prior_ref):
    state = jnp.zeros((ROWS, HD), F32)
    for c in range(pay_ref.shape[0]):
        out_ref[c] = state.astype(BF16)
        prior_ref[c] = state
        decay = jnp.exp(joined_rows(pay_ref[c, ROWS:]))
        decay_ref[c : c + 1] = decay
        state = decay * state + pay_ref[c, :ROWS].astype(F32)


def forward_split_kernel(half, loc_ref, got_ref, cumt_ref, scanned_ref, mine_ref, theirs_ref):
    core = lax.axis_index("core")
    for h in range(half):
        log0, _ = pair_logs(core, half, h, cumt_ref, got_ref)
        state0, _ = pair_values(core, half, h, loc_ref, got_ref)
        prior0 = scanned_ref[h].astype(F32)
        prior1 = jnp.exp(log0) * prior0 + state0
        mine_ref[h] = one_of(core == 0, prior0, prior1).astype(BF16)
        theirs_ref[h] = one_of(core == 0, prior1, prior0).astype(BF16)


def backward_join_kernel(half, out_ref, got_ref, gain_ref, cumt_ref, got_state_ref, pay_ref):
    core = lax.axis_index("core")
    for h in range(half):
        log0, _ = pair_logs(core, half, h, cumt_ref, got_state_ref)
        state0, state1 = pair_values(core, half, h, out_ref, got_ref)
        both = state0 + jnp.exp(log0) * state1
        own = one_of(core == 0, gain_ref[h : h + 1], gain_ref[half + h : half + h + 1])
        rows = small_rows(own + got_ref[h, HD : HD + 1])
        put_chunks(pay_ref, h, both.astype(BF16), rows)


def backward_scan_kernel(pay_ref, decay_ref, prior_ref, out_ref):
    state = jnp.zeros((ROWS, HD), F32)
    total = jnp.zeros((1, HD), F32)
    meets = {}
    for c in reversed(range(pay_ref.shape[0])):
        out_ref[c, :ROWS] = state.astype(BF16)
        meets[c] = jnp.sum(state * prior_ref[c], axis=0, keepdims=True)
        state = decay_ref[c : c + 1] * state + pay_ref[c, :ROWS].astype(F32)
        total = total + joined_rows(pay_ref[c, ROWS:])
    for c in range(pay_ref.shape[0]):
        out_ref[c, ROWS:] = small_rows(total, meets[c])


def backward_split_kernel(
    half, out_ref, got_ref, loc_ref, cumt_ref, got_state_ref, prior_ref, back_ref, mine_ref, theirs_ref
):
    core = lax.axis_index("core")
    parts = HD // ROWS
    for h in range(half):
        log0, log1 = pair_logs(core, half, h, cumt_ref, got_state_ref)
        _, state1 = pair_values(core, half, h, out_ref, got_ref)
        state0, _ = pair_values(core, half, h, loc_ref, got_state_ref)
        later1 = jnp.concatenate([back_ref[h * parts + part, :ROWS] for part in range(parts)])
        later1 = later1.astype(F32)
        later0 = jnp.exp(log1) * later1 + state1
        mine_ref[h, :HD] = one_of(core == 0, later0, later1).astype(BF16)
        theirs_ref[h, :HD] = one_of(core == 0, later1, later0).astype(BF16)
        meet = sum(joined_rows(back_ref[h * parts + part, ROWS:], 1) for part in range(parts))
        meet = jnp.exp(log0 + log1) * meet
        prior = prior_ref[h].astype(F32)
        meet0 = meet + jnp.exp(log0) * jnp.sum(state1 * prior, axis=0, keepdims=True)
        meet1 = meet + jnp.exp(log1) * jnp.sum(later1 * state0, axis=0, keepdims=True)
        gain = joined_rows(back_ref[h * parts, ROWS:])
        mine_ref[h, HD:] = small_rows(gain, one_of(core == 0, meet0, meet1))
        theirs_ref[h, HD:] = small_rows(gain, one_of(core == 0, meet1, meet0))


def within_kernel(heads, q_ref, k_ref, v_ref, cum_ref, cumt_ref, intra_ref, weights_ref, decayed_ref):
    length = q_ref.shape[0]
    half = length // 2
    cum = cum_ref[...]
    for h in range(heads):
        cols = slice(h * HD, (h + 1) * HD)
        q, k, v = q_ref[:, cols], k_ref[:, cols], v_ref[:, cols]
        top, bottom = decay_blocks(cum[:, h : h + 1], cumt_ref[h : h + 1])
        top = (top * dot(q[:half], k[:half], (1, 1))).astype(BF16)
        bottom = (bottom * dot(q[half:], k, (1, 1))).astype(BF16)
        weights_ref[h, :half, :half] = top
        weights_ref[h, :half, half:] = jnp.zeros((half, length - half), BF16)
        weights_ref[h, half:] = bottom
        decayed_ref[:, cols] = (q.astype(F32) * jnp.exp(cum[:, h : h + 1])).astype(BF16)
        intra_ref[:half, cols] = dot(top, v[:half])
        intra_ref[half:, cols] = dot(bottom, v)


def gate_kernel(gate_ref, cot_ref, gain_ref, opened_ref, upstream_ref):
    opened = jax.nn.sigmoid(gate_ref[...].astype(F32))
    opened_ref[...] = opened
    upstream_ref[...] = cot_ref[...].astype(F32) * opened * gain_ref[...]


def attention_kernel(
    heads, decayed_ref, intra_ref, upstream_ref, mine_ref, got_ref, attn_ref, prior_ref, sums_ref
):
    length = decayed_ref.shape[0]
    core = lax.axis_index("core")
    half = heads // 2
    prior_ref[pl.ds(core * half, half)] = mine_ref[...]
    prior_ref[pl.ds((1 - core) * half, half)] = got_ref[...]
    squares = jnp.zeros((length, HD), F32)
    cross = jnp.zeros((length, HD), F32)
    for h in range(heads):
        cols = slice(h * HD, (h + 1) * HD)
        attn = dot(decayed_ref[:, cols], prior_ref[h]) + intra_ref[:, cols]
        attn_ref[:, cols] = attn
        squares = squares + attn * attn
        cross = cross + upstream_ref[:, cols] * attn
    sums_ref[...] = jnp.concatenate(
        [
            jnp.sum(squares.T, axis=0, keepdims=True),
            jnp.sum(cross.T, axis=0, keepdims=True),
            jnp.zeros((6, length), F32),
        ]
    )


def norm_kernel(
    heads, full_width, decayed_ref, cot_ref, opened_ref, upstream_ref, attn_ref,
    sums0_ref, sums1_ref, sums2_ref, sums3_ref, grad_ref, out_ref, theirs_ref, gain_ref, inverse_ref,
):
    length = decayed_ref.shape[0]
    half = heads // 2
    core = lax.axis_index("core")
    sums = sums0_ref[...] + sums1_ref[...] + sums2_ref[...] + sums3_ref[...]
    inverse_row = 1.0 / jnp.sqrt(sums[0:1] / full_width + EPSILON)
    cross_row = sums[1:2] * inverse_row / full_width
    inverse = jnp.broadcast_to(inverse_row, (HD, length)).T
    cross = jnp.broadcast_to(cross_row, (HD, length)).T
    inverse_ref[...] = inverse
    for h in range(heads):
        cols = slice(h * HD, (h + 1) * HD)
        normalized = attn_ref[:, cols] * inverse
        through = cot_ref[:, cols].astype(F32) * opened_ref[:, cols]
        gain_ref[h : h + 1] = jnp.sum(through * normalized, axis=0, keepdims=True)
        grad = ((upstream_ref[:, cols] - normalized * cross) * inverse).astype(BF16)
        grad_ref[:, cols] = grad
        out_ref[h] = dot(decayed_ref[:, cols], grad, (0, 0))
    theirs_ref[:, :HD] = out_ref[pl.ds((1 - core) * half, half)]
    for h in range(half):
        value = one_of(core == 0, gain_ref[half + h : half + h + 1], gain_ref[h : h + 1])
        theirs_ref[h, HD:] = jnp.broadcast_to(value, (EXTRA, HD))


def finish_kernel(
    heads, opened_ref, upstream_ref, gain_ref, attn_ref, inverse_ref, attended_ref, ggate_ref
):
    for h in range(heads):
        cols = slice(h * HD, (h + 1) * HD)
        opened = opened_ref[:, cols]
        normalized = attn_ref[:, cols] * inverse_ref[...]
        attended_ref[:, cols] = (normalized * gain_ref[:, cols] * opened).astype(BF16)
        ggate_ref[:, cols] = (upstream_ref[:, cols] * normalized * (1.0 - opened)).astype(BF16)


def query_gradient_kernel(
    heads, k_ref, v_ref, cum_ref, cumt_ref, grad_ref, prior_ref, gq_ref, mixed_ref
):
    length = k_ref.shape[0]
    half = length // 2
    cum = cum_ref[...]
    for h in range(heads):
        cols = slice(h * HD, (h + 1) * HD)
        k, v, grad = k_ref[:, cols], v_ref[:, cols], grad_ref[:, cols]
        top, bottom = decay_blocks(cum[:, h : h + 1], cumt_ref[h : h + 1])
        top = (top * dot(grad[:half], v[:half], (1, 1))).astype(BF16)
        bottom = (bottom * dot(grad[half:], v, (1, 1))).astype(BF16)
        mixed_ref[h, :half, :half] = top
        mixed_ref[h, :half, half:] = jnp.zeros((half, length - half), BF16)
        mixed_ref[h, half:] = bottom
        gq = jnp.concatenate([dot(top, k[:half]), dot(bottom, k)])
        gq = gq + jnp.exp(cum[:, h : h + 1]) * dot(grad, prior_ref[h], (1, 1))
        gq_ref[:, cols] = gq.astype(BF16)


def key_part_kernel(heads, q_ref, grad_ref, weights_ref, mixed_ref, gk_ref, gv_ref):
    for h in range(heads):
        cols = slice(h * HD, (h + 1) * HD)
        gk_ref[:, cols] = dot(mixed_ref[h], q_ref[:, cols], (0, 0))
        gv_ref[:, cols] = dot(weights_ref[h], grad_ref[:, cols], (0, 0))


def key_gradient_kernel(
    heads, k_ref, v_ref, cum_ref, attn_ref, grad_ref, gk_part_ref, gv_part_ref, mine_ref,
    got_ref, gk_ref, gv_ref, gdecayt_ref, ggain_ref, later_ref,
):
    length = k_ref.shape[0]
    half = heads // 2
    core = lax.axis_index("core")
    later_ref[pl.ds(core * half, half)] = mine_ref[:, :HD]
    later_ref[pl.ds((1 - core) * half, half)] = got_ref[:, :HD]
    cum = cum_ref[...]
    last = cum[length - 1 : length]
    lane = lax.broadcasted_iota(jnp.int32, (length, HD), 1)
    tails = []
    changes = jnp.zeros((length, HD), F32)
    for h in range(heads):
        cols = slice(h * HD, (h + 1) * HD)
        k, v, grad, later = k_ref[:, cols], v_ref[:, cols], grad_ref[:, cols], later_ref[h]
        mine, got = mine_ref[h % half, HD:], got_ref[h % half, HD:]
        own = core == h // half
        ggain_ref[:, cols] = one_of(own, joined_rows(mine), joined_rows(got))
        fade = jnp.exp(last[:, h : h + 1] - cum[:, h : h + 1])
        pull = fade * dot(v, later, (1, 1))
        gk_part = gk_part_ref[:, cols]
        gk_ref[:, cols] = (gk_part + pull).astype(BF16)
        gv_ref[:, cols] = (gv_part_ref[:, cols] + fade * dot(k, later)).astype(BF16)
        key = k.astype(F32)
        pulled = key * pull
        meet = one_of(own, joined_rows(mine, 1), joined_rows(got, 1))
        tails.append(meet + jnp.sum(pulled, axis=0, keepdims=True))
        change = attn_ref[:, cols] * grad.astype(F32) - key * gk_part - pulled
        changes = jnp.where(lane == h, jnp.sum(change, axis=1, keepdims=True), changes)
    tail = jnp.sum(jnp.concatenate(tails), axis=1, keepdims=True)
    ones = triangle_bf(length)
    gdecayt_ref[...] = tail + sum(dot(part, ones) for part in three_parts(changes.T[:heads]))


def local_call(kernel, outs, args, flops=0, moved=0, scratch=()):
    return pl.pallas_call(
        kernel,
        out_shape=[jax.ShapeDtypeStruct(shape, kind) for shape, kind in outs],
        scratch_shapes=list(scratch),
        compiler_params=pltpu.CompilerParams(vmem_limit_bytes=40 * 2**20),
        cost_estimate=pl.CostEstimate(flops=flops, bytes_accessed=moved, transcendentals=0),
    )(*args)


def exchange(payload):
    return lax.all_to_all(payload, ("x", "z"), 0, 0, tiled=True)


def swap(value):
    return lax.ppermute(value, "core", [(0, 1), (1, 0)])


def per_device(queries, key_rows, value_rows, gate_logits, norm_gain, log_decay, cotangent):
    length, width = queries.shape
    heads = log_decay.shape[1]
    half = heads // 2
    chips = lax.axis_size("x") * lax.axis_size("z")
    size = lax.axis_size("head")
    full_width = width * size
    gain = norm_gain.reshape(1, width)
    state, part_state = (heads, HD, HD), (half, HD, HD)
    carried = (half, HD + EXTRA, HD)
    chunks = half * HD // ROWS
    tokens, tokens32 = ((length, width), BF16), ((length, width), F32)
    square = ((heads, length, length), BF16)
    local, theirs, cum, cumt = local_call(
        functools.partial(local_state_kernel, heads),
        [(state, BF16), (carried, BF16), ((length, heads), F32), ((heads, length), F32)],
        (key_rows, value_rows, log_decay.T),
        WORK, WORK // 100,
    )
    got = swap(theirs)
    intra, weights, decayed = local_call(
        functools.partial(within_kernel, heads),
        [tokens32, square, tokens],
        (queries, key_rows, value_rows, cum, cumt),
        WORK, WORK // 100,
    )
    got, intra = lax.optimization_barrier((got, intra))
    (payload,) = local_call(
        functools.partial(forward_join_kernel, half),
        [((chunks, ROWS + EXTRA, HD), BF16)],
        (local, got, cumt),
    )
    scanned, decays, chip_prior = local_call(
        forward_scan_kernel,
        [((chips, ROWS, HD), BF16), ((chips, HD), F32), ((chips, ROWS, HD), F32)],
        (exchange(payload),),
    )
    scanned = exchange(scanned).reshape(part_state)
    mine, theirs = local_call(
        functools.partial(forward_split_kernel, half),
        [(part_state, BF16)] * 2,
        (local, got, cumt, scanned),
    )
    opened, upstream = local_call(
        gate_kernel, [tokens32] * 2, (gate_logits, cotangent, gain), WORK, WORK // 100
    )
    attn, prior, sums = local_call(
        functools.partial(attention_kernel, heads),
        [tokens32, (state, BF16), ((8, length), F32)],
        (decayed, intra, upstream, mine, swap(theirs)),
        WORK, WORK // 100,
    )
    others = [
        lax.ppermute(sums, "head", [(i, i ^ step) for i in range(size)])
        for step in range(1, size)
    ]
    grad, outgoing, theirs, gains, inverse = local_call(
        functools.partial(norm_kernel, heads, full_width),
        [tokens, (state, F32), (carried, F32), ((heads, HD), F32), ((length, HD), F32)],
        (decayed, cotangent, opened, upstream, attn, sums, *others),
        WORK, WORK // 100,
    )
    got_back = swap(theirs)
    attended, grad_gate = local_call(
        functools.partial(finish_kernel, heads),
        [tokens] * 2,
        (opened, upstream, gain, attn, inverse),
        WORK, WORK // 100,
    )
    grad_q, mixed = local_call(
        functools.partial(query_gradient_kernel, heads),
        [tokens, square],
        (key_rows, value_rows, cum, cumt, grad, prior),
        WORK, WORK // 100,
    )
    got_back, mixed = lax.optimization_barrier((got_back, mixed))
    (payload,) = local_call(
        functools.partial(backward_join_kernel, half),
        [((chunks, ROWS + EXTRA, HD), BF16)],
        (outgoing, got_back, gains, cumt, got),
    )
    (back,) = local_call(
        backward_scan_kernel,
        [((chips, ROWS + EXTRA, HD), BF16)],
        (exchange(payload), decays, chip_prior),
    )
    mine, theirs = local_call(
        functools.partial(backward_split_kernel, half),
        [(carried, BF16)] * 2,
        (outgoing, got_back, local, cumt, got, scanned, exchange(back)),
    )
    gk_part, gv_part = local_call(
        functools.partial(key_part_kernel, heads),
        [tokens32] * 2,
        (queries, grad, weights, mixed),
        WORK, WORK // 100,
    )
    grad_k, grad_v, grad_decay, grad_gain = local_call(
        functools.partial(key_gradient_kernel, heads),
        [tokens, tokens, ((heads, length), F32), ((1, width), F32)],
        (key_rows, value_rows, cum, attn, grad, gk_part, gv_part, mine, swap(theirs)),
        WORK, WORK // 100,
        [pltpu.VMEM(state, BF16)],
    )
    return attended, grad_q, grad_k, grad_v, grad_gate, grad_decay.T, grad_gain.reshape(width)


def solution(mesh):
    fine = Mesh(mesh.devices.reshape(4, 8, 2, 4), ("x", "z", "core", "head"))
    tokens = P(("x", "z", "core"), "head")
    return jax.shard_map(
        per_device,
        mesh=fine,
        in_specs=(tokens, tokens, tokens, tokens, P("head"), tokens, tokens),
        out_specs=(tokens, tokens, tokens, tokens, tokens, tokens, P("head")),
        check_vma=False,
    )
```

```python
import functools

import jax
import jax.numpy as jnp
from jax import lax
from jax.experimental import pallas as pl
from jax.experimental.pallas import tpu as pltpu
from jax.sharding import Mesh
from jax.sharding import PartitionSpec as P

EPSILON = 1e-05
HD = 128
ROWS = 16
EXTRA = 8
F32 = jnp.float32
BF16 = jnp.bfloat16
NEGATIVE = -1e30
WORK = 500_000_000


def dot(a, b, contract=(1, 0)):
    dims = (((contract[0],), (contract[1],)), ((), ()))
    return lax.dot_general(a, b, dims, preferred_element_type=F32)


def three_parts(value):
    high = value.astype(BF16)
    rest = value - high.astype(F32)
    middle = rest.astype(BF16)
    low = (rest - middle.astype(F32)).astype(BF16)
    return high, middle, low


def triangle_bf(length, flipped=False):
    row = lax.broadcasted_iota(jnp.int32, (length, length), 0)
    col = lax.broadcasted_iota(jnp.int32, (length, length), 1)
    return jnp.where(row <= col if flipped else col <= row, 1.0, 0.0).astype(BF16)


def exact_sums(ones, value):
    return sum(dot(ones, part) for part in three_parts(value))


def small_rows(*values):
    row = lax.broadcasted_iota(jnp.int32, (EXTRA, HD), 0)
    block = jnp.zeros((EXTRA, HD), F32)
    for place, value in enumerate(values):
        for turn, part in enumerate(three_parts(value)):
            block = jnp.where(row == 3 * place + turn, part.astype(F32), block)
    return block.astype(BF16)


def joined_rows(block, place=0):
    block = block[...].astype(F32)
    at = 3 * place
    return block[at : at + 1] + block[at + 1 : at + 2] + block[at + 2 : at + 3]


def masked_gap(cum_col, cum_row, low, high, left, right):
    gap = cum_col[low:high] - cum_row[:, left:right]
    if right <= low:
        return gap
    row = lax.broadcasted_iota(jnp.int32, gap.shape, 0) + low
    col = lax.broadcasted_iota(jnp.int32, gap.shape, 1) + left
    return jnp.where(col <= row, gap, NEGATIVE)


def decay_blocks(cum_col, cum_row):
    length = cum_col.shape[0]
    half = length // 2
    top = jnp.exp(masked_gap(cum_col, cum_row, 0, half, 0, half))
    bottom = jnp.exp(masked_gap(cum_col, cum_row, half, length, 0, length))
    return top, bottom


def one_of(first, if_first, if_second):
    return jnp.where(first, if_first, if_second)


def local_state_kernel(heads, k_ref, v_ref, ldt_ref, loc_ref, theirs_ref, cum_ref, cumt_ref):
    length = k_ref.shape[0]
    half = heads // 2
    core = lax.axis_index("core")
    ones = triangle_bf(length, True)
    cumt = sum(dot(part, ones) for part in three_parts(ldt_ref[...]))
    cumt_ref[...] = cumt
    cum = jnp.concatenate([cumt, jnp.zeros((HD - heads, length), F32)]).T[:, :heads]
    cum_ref[...] = cum
    last = cum[length - 1 : length]
    fade = jnp.exp(last - cum)
    for h in range(heads):
        cols = slice(h * HD, (h + 1) * HD)
        decayed = (k_ref[:, cols].astype(F32) * fade[:, h : h + 1]).astype(BF16)
        loc_ref[h] = dot(decayed, v_ref[:, cols], (0, 0)).astype(BF16)
    theirs_ref[:, :HD] = loc_ref[pl.ds((1 - core) * half, half)]
    for h in range(half):
        value = one_of(core == 0, last[:, half + h : half + h + 1], last[:, h : h + 1])
        theirs_ref[h, HD:] = small_rows(jnp.broadcast_to(value, (1, HD)))


class Outward:
    def __init__(self, place, held, sems, base):
        self.place, self.held, self.sems, self.base, self.copies = place, held, sems, base, []

    def put(self, h, value):
        cols = slice(h * HD, (h + 1) * HD)
        self.held[h] = value
        copy = pltpu.make_async_copy(self.held.at[h], self.place.at[:, cols], self.sems.at[self.base + h])
        copy.start()
        self.copies.append(copy)

    def wait(self):
        for copy in self.copies:
            copy.wait()


def pair_logs(core, half, h, cumt_ref, got_ref):
    length = cumt_ref.shape[1]
    own = one_of(
        core == 0, cumt_ref[h : h + 1, length - 1 :], cumt_ref[half + h : half + h + 1, length - 1 :]
    )
    own = jnp.broadcast_to(own, (1, HD))
    other = joined_rows(got_ref[h, HD:])
    return one_of(core == 0, own, other), one_of(core == 0, other, own)


def pair_values(core, half, h, loc_ref, got_ref):
    own = loc_ref[core * half + h].astype(F32)
    other = got_ref[h, :HD].astype(F32)
    return one_of(core == 0, own, other), one_of(core == 0, other, own)


def put_chunks(pay_ref, h, state, rows):
    parts = HD // ROWS
    for part in range(parts):
        pay_ref[h * parts + part, :ROWS] = state[part * ROWS : (part + 1) * ROWS]
        pay_ref[h * parts + part, ROWS:] = rows


def forward_join_kernel(half, loc_ref, got_ref, cumt_ref, pay_ref):
    core = lax.axis_index("core")
    for h in range(half):
        log0, log1 = pair_logs(core, half, h, cumt_ref, got_ref)
        state0, state1 = pair_values(core, half, h, loc_ref, got_ref)
        both = jnp.exp(log1) * state0 + state1
        put_chunks(pay_ref, h, both.astype(BF16), small_rows(log0 + log1))


def forward_scan_kernel(pay_ref, out_ref, decay_ref, prior_ref):
    state = jnp.zeros((ROWS, HD), F32)
    for c in range(pay_ref.shape[0]):
        out_ref[c] = state.astype(BF16)
        prior_ref[c] = state
        decay = jnp.exp(joined_rows(pay_ref[c, ROWS:]))
        decay_ref[c : c + 1] = decay
        state = decay * state + pay_ref[c, :ROWS].astype(F32)


def forward_split_kernel(half, loc_ref, got_ref, cumt_ref, scanned_ref, mine_ref, theirs_ref):
    core = lax.axis_index("core")
    for h in range(half):
        log0, _ = pair_logs(core, half, h, cumt_ref, got_ref)
        state0, _ = pair_values(core, half, h, loc_ref, got_ref)
        prior0 = scanned_ref[h].astype(F32)
        prior1 = jnp.exp(log0) * prior0 + state0
        mine_ref[h] = one_of(core == 0, prior0, prior1).astype(BF16)
        theirs_ref[h] = one_of(core == 0, prior1, prior0).astype(BF16)


def backward_join_kernel(half, out_ref, got_ref, gain_ref, cumt_ref, got_state_ref, pay_ref):
    core = lax.axis_index("core")
    for h in range(half):
        log0, _ = pair_logs(core, half, h, cumt_ref, got_state_ref)
        state0, state1 = pair_values(core, half, h, out_ref, got_ref)
        both = state0 + jnp.exp(log0) * state1
        own = one_of(core == 0, gain_ref[h : h + 1], gain_ref[half + h : half + h + 1])
        rows = small_rows(own + got_ref[h, HD : HD + 1])
        put_chunks(pay_ref, h, both.astype(BF16), rows)


def backward_scan_kernel(pay_ref, decay_ref, prior_ref, out_ref):
    state = jnp.zeros((ROWS, HD), F32)
    total = jnp.zeros((1, HD), F32)
    meets = {}
    for c in reversed(range(pay_ref.shape[0])):
        out_ref[c, :ROWS] = state.astype(BF16)
        meets[c] = jnp.sum(state * prior_ref[c], axis=0, keepdims=True)
        state = decay_ref[c : c + 1] * state + pay_ref[c, :ROWS].astype(F32)
        total = total + joined_rows(pay_ref[c, ROWS:])
    for c in range(pay_ref.shape[0]):
        out_ref[c, ROWS:] = small_rows(total, meets[c])


def backward_split_kernel(
    half, out_ref, got_ref, loc_ref, cumt_ref, got_state_ref, prior_ref, back_ref, mine_ref, theirs_ref
):
    core = lax.axis_index("core")
    parts = HD // ROWS
    for h in range(half):
        log0, log1 = pair_logs(core, half, h, cumt_ref, got_state_ref)
        _, state1 = pair_values(core, half, h, out_ref, got_ref)
        state0, _ = pair_values(core, half, h, loc_ref, got_state_ref)
        later1 = jnp.concatenate([back_ref[h * parts + part, :ROWS] for part in range(parts)])
        later1 = later1.astype(F32)
        later0 = jnp.exp(log1) * later1 + state1
        mine_ref[h, :HD] = one_of(core == 0, later0, later1).astype(BF16)
        theirs_ref[h, :HD] = one_of(core == 0, later1, later0).astype(BF16)
        meet = sum(joined_rows(back_ref[h * parts + part, ROWS:], 1) for part in range(parts))
        meet = jnp.exp(log0 + log1) * meet
        prior = prior_ref[h].astype(F32)
        meet0 = meet + jnp.exp(log0) * jnp.sum(state1 * prior, axis=0, keepdims=True)
        meet1 = meet + jnp.exp(log1) * jnp.sum(later1 * state0, axis=0, keepdims=True)
        gain = joined_rows(back_ref[h * parts, ROWS:])
        mine_ref[h, HD:] = small_rows(gain, one_of(core == 0, meet0, meet1))
        theirs_ref[h, HD:] = small_rows(gain, one_of(core == 0, meet1, meet0))


def within_kernel(heads, q_ref, k_ref, v_ref, cum_ref, cumt_ref, intra_ref, weights_ref, decayed_ref):
    length = q_ref.shape[0]
    half = length // 2
    cum = cum_ref[...]
    grown = jnp.exp(cum)
    for h in range(heads):
        cols = slice(h * HD, (h + 1) * HD)
        q, k, v = q_ref[:, cols], k_ref[:, cols], v_ref[:, cols]
        top, bottom = decay_blocks(cum[:, h : h + 1], cumt_ref[h : h + 1])
        top = (top * dot(q[:half], k[:half], (1, 1))).astype(BF16)
        bottom = (bottom * dot(q[half:], k, (1, 1))).astype(BF16)
        weights_ref[h, :half, :half] = top
        weights_ref[h, :half, half:] = jnp.zeros((half, length - half), BF16)
        weights_ref[h, half:] = bottom
        decayed_ref[:, cols] = (q.astype(F32) * grown[:, h : h + 1]).astype(BF16)
        intra_ref[:half, cols] = dot(top, v[:half])
        intra_ref[half:, cols] = dot(bottom, v)


def gate_kernel(gate_ref, cot_ref, gain_ref, opened_ref, upstream_ref):
    opened = jax.nn.sigmoid(gate_ref[...].astype(F32))
    opened_ref[...] = opened
    upstream_ref[...] = cot_ref[...].astype(F32) * opened * gain_ref[...]


def attention_kernel(
    heads, decayed_ref, intra_ref, upstream_ref, mine_ref, got_ref, attn_ref, prior_ref, sums_ref
):
    length = decayed_ref.shape[0]
    core = lax.axis_index("core")
    half = heads // 2
    prior_ref[pl.ds(core * half, half)] = mine_ref[...]
    prior_ref[pl.ds((1 - core) * half, half)] = got_ref[...]
    squares = jnp.zeros((length, HD), F32)
    cross = jnp.zeros((length, HD), F32)
    for h in range(heads):
        cols = slice(h * HD, (h + 1) * HD)
        attn = dot(decayed_ref[:, cols], prior_ref[h]) + intra_ref[:, cols]
        attn_ref[:, cols] = attn
        squares = squares + attn * attn
        cross = cross + upstream_ref[:, cols] * attn
    sums_ref[...] = jnp.concatenate(
        [
            jnp.sum(squares.T, axis=0, keepdims=True),
            jnp.sum(cross.T, axis=0, keepdims=True),
            jnp.zeros((6, length), F32),
        ]
    )


def norm_kernel(
    heads, full_width, decayed_ref, cot_ref, opened_ref, upstream_ref, attn_ref,
    sums0_ref, sums1_ref, sums2_ref, sums3_ref, grad_ref, out_ref, theirs_ref, gain_ref, inverse_ref,
):
    length = decayed_ref.shape[0]
    half = heads // 2
    core = lax.axis_index("core")
    sums = sums0_ref[...] + sums1_ref[...] + sums2_ref[...] + sums3_ref[...]
    inverse_row = 1.0 / jnp.sqrt(sums[0:1] / full_width + EPSILON)
    cross_row = sums[1:2] * inverse_row / full_width
    inverse = jnp.broadcast_to(inverse_row, (HD, length)).T
    cross = jnp.broadcast_to(cross_row, (HD, length)).T
    inverse_ref[...] = inverse
    for h in range(heads):
        cols = slice(h * HD, (h + 1) * HD)
        normalized = attn_ref[:, cols] * inverse
        through = cot_ref[:, cols].astype(F32) * opened_ref[:, cols]
        gain_ref[h : h + 1] = jnp.sum(through * normalized, axis=0, keepdims=True)
        grad = ((upstream_ref[:, cols] - normalized * cross) * inverse).astype(BF16)
        grad_ref[:, cols] = grad
        out_ref[h] = dot(decayed_ref[:, cols], grad, (0, 0))
    theirs_ref[:, :HD] = out_ref[pl.ds((1 - core) * half, half)]
    for h in range(half):
        value = one_of(core == 0, gain_ref[half + h : half + h + 1], gain_ref[h : h + 1])
        theirs_ref[h, HD:] = jnp.broadcast_to(value, (EXTRA, HD))


def finish_kernel(
    heads, opened_ref, upstream_ref, gain_ref, attn_ref, inverse_ref, attended_hbm, ggate_hbm,
    attended_ref, ggate_ref, sems,
):
    attended = Outward(attended_hbm, attended_ref, sems, 0)
    ggate = Outward(ggate_hbm, ggate_ref, sems, heads)
    for h in range(heads):
        cols = slice(h * HD, (h + 1) * HD)
        opened = opened_ref[:, cols]
        normalized = attn_ref[:, cols] * inverse_ref[...]
        attended.put(h, (normalized * gain_ref[:, cols] * opened).astype(BF16))
        ggate.put(h, (upstream_ref[:, cols] * normalized * (1.0 - opened)).astype(BF16))
    attended.wait()
    ggate.wait()


def query_gradient_kernel(
    heads, q_ref, k_ref, v_ref, cum_ref, cumt_ref, grad_ref, prior_ref, weights_ref,
    gq_hbm, gk_ref, gv_ref, gq_ref, mixed_ref, sems,
):
    length = k_ref.shape[0]
    half = length // 2
    cum = cum_ref[...]
    grown = jnp.exp(cum)
    copies = []
    for low in (half, 0):
        rows, seen = slice(low, low + half), slice(0, low + half)
        for h in range(heads):
            cols = slice(h * HD, (h + 1) * HD)
            grad = grad_ref[rows, cols]
            gap = masked_gap(cum[:, h : h + 1], cumt_ref[h : h + 1], low, low + half, 0, low + half)
            mixed = (jnp.exp(gap) * dot(grad, v_ref[seen, cols], (1, 1))).astype(BF16)
            mixed_ref[h, rows, seen] = mixed
            gq = dot(mixed, k_ref[seen, cols])
            gq = gq + grown[rows, h : h + 1] * dot(grad, prior_ref[h], (1, 1))
            gq_ref[rows, cols] = gq.astype(BF16)
        copy = pltpu.make_async_copy(gq_ref.at[rows], gq_hbm.at[rows], sems.at[len(copies)])
        copy.start()
        copies.append(copy)
    top, bottom = slice(0, half), slice(half, length)
    for h in range(heads):
        cols = slice(h * HD, (h + 1) * HD)
        for held_ref, by_ref, out_ref in ((mixed_ref, q_ref, gk_ref), (weights_ref, grad_ref, gv_ref)):
            early = dot(held_ref[h, top, top], by_ref[top, cols], (0, 0))
            late = dot(held_ref[h, bottom], by_ref[bottom, cols], (0, 0))
            out_ref[top, cols] = early + late[:half]
            out_ref[bottom, cols] = late[half:]
    for copy in copies:
        copy.wait()


def key_gradient_kernel(
    heads, k_ref, v_ref, cum_ref, attn_ref, grad_ref, gk_part_ref, gv_part_ref, mine_ref,
    got_ref, gk_ref, gv_ref, gdecayt_ref, ggain_ref, later_ref,
):
    length = k_ref.shape[0]
    half = heads // 2
    core = lax.axis_index("core")
    later_ref[pl.ds(core * half, half)] = mine_ref[:, :HD]
    later_ref[pl.ds((1 - core) * half, half)] = got_ref[:, :HD]
    cum = cum_ref[...]
    last = cum[length - 1 : length]
    lane = lax.broadcasted_iota(jnp.int32, (length, HD), 1)
    tails = []
    fades = jnp.exp(last - cum)
    changes = jnp.zeros((length, HD), F32)
    for h in range(heads):
        cols = slice(h * HD, (h + 1) * HD)
        k, v, grad, later = k_ref[:, cols], v_ref[:, cols], grad_ref[:, cols], later_ref[h]
        mine, got = mine_ref[h % half, HD:], got_ref[h % half, HD:]
        own = core == h // half
        ggain_ref[:, cols] = one_of(own, joined_rows(mine), joined_rows(got))
        fade = fades[:, h : h + 1]
        pull = fade * dot(v, later, (1, 1))
        gk_part = gk_part_ref[:, cols]
        gk_ref[:, cols] = (gk_part + pull).astype(BF16)
        gv_ref[:, cols] = (gv_part_ref[:, cols] + fade * dot(k, later)).astype(BF16)
        key = k.astype(F32)
        pulled = key * pull
        meet = one_of(own, joined_rows(mine, 1), joined_rows(got, 1))
        tails.append(meet + jnp.sum(pulled, axis=0, keepdims=True))
        change = attn_ref[:, cols] * grad.astype(F32) - key * gk_part - pulled
        changes = jnp.where(lane == h, jnp.sum(change, axis=1, keepdims=True), changes)
    tail = jnp.sum(jnp.concatenate(tails), axis=1, keepdims=True)
    ones = triangle_bf(length)
    gdecayt_ref[...] = tail + sum(dot(part, ones) for part in three_parts(changes.T[:heads]))


def local_call(kernel, outs, args, flops=0, moved=0, scratch=(), far_out=(), room=40):
    def spec(far):
        return pl.BlockSpec(memory_space=pltpu.HBM if far else pltpu.VMEM)

    return pl.pallas_call(
        kernel,
        out_shape=[jax.ShapeDtypeStruct(shape, kind) for shape, kind in outs],
        in_specs=[spec(False)] * len(args),
        out_specs=[spec(place in far_out) for place in range(len(outs))],
        scratch_shapes=list(scratch),
        compiler_params=pltpu.CompilerParams(vmem_limit_bytes=int(room * 2**20)),
        cost_estimate=pl.CostEstimate(flops=flops, bytes_accessed=moved, transcendentals=0),
    )(*args)


def exchange(payload):
    return lax.all_to_all(payload, ("x", "z"), 0, 0, tiled=True)


def swap(value):
    return lax.ppermute(value, "core", [(0, 1), (1, 0)])


def per_device(queries, key_rows, value_rows, gate_logits, norm_gain, log_decay, cotangent):
    length, width = queries.shape
    heads = log_decay.shape[1]
    half = heads // 2
    chips = lax.axis_size("x") * lax.axis_size("z")
    size = lax.axis_size("head")
    full_width = width * size
    gain = norm_gain.reshape(1, width)
    state, part_state = (heads, HD, HD), (half, HD, HD)
    carried = (half, HD + EXTRA, HD)
    chunks = half * HD // ROWS
    tokens, tokens32 = ((length, width), BF16), ((length, width), F32)
    square = ((heads, length, length), BF16)
    held = pltpu.VMEM((heads, length, HD), BF16)
    local, theirs, cum, cumt = local_call(
        functools.partial(local_state_kernel, heads),
        [(state, BF16), (carried, BF16), ((length, heads), F32), ((heads, length), F32)],
        (key_rows, value_rows, log_decay.T),
        WORK, WORK // 100,
        room=53.2,
    )
    got = swap(theirs)
    intra, weights, decayed = local_call(
        functools.partial(within_kernel, heads),
        [tokens32, square, tokens],
        (queries, key_rows, value_rows, cum, cumt),
        WORK, WORK // 100,
    )
    (payload,) = local_call(
        functools.partial(forward_join_kernel, half),
        [((chunks, ROWS + EXTRA, HD), BF16)],
        (local, got, cumt),
    )
    scanned, decays, chip_prior = local_call(
        forward_scan_kernel,
        [((chips, ROWS, HD), BF16), ((chips, HD), F32), ((chips, ROWS, HD), F32)],
        (exchange(payload),),
    )
    scanned = exchange(scanned).reshape(part_state)
    mine, theirs = local_call(
        functools.partial(forward_split_kernel, half),
        [(part_state, BF16)] * 2,
        (local, got, cumt, scanned),
    )
    opened, upstream = local_call(
        gate_kernel, [tokens32] * 2, (gate_logits, cotangent, gain), WORK, WORK // 100
    )
    attn, prior, sums = local_call(
        functools.partial(attention_kernel, heads),
        [tokens32, (state, BF16), ((8, length), F32)],
        (decayed, intra, upstream, mine, swap(theirs)),
        WORK, WORK // 100,
    )
    others = [
        lax.ppermute(sums, "head", [(i, i ^ step) for i in range(size)])
        for step in range(1, size)
    ]
    grad, outgoing, theirs, gains, inverse = local_call(
        functools.partial(norm_kernel, heads, full_width),
        [tokens, (state, F32), (carried, F32), ((heads, HD), F32), ((length, HD), F32)],
        (decayed, cotangent, opened, upstream, attn, sums, *others),
        WORK, WORK // 100,
    )
    got_back = swap(theirs)
    attended, grad_gate = local_call(
        functools.partial(finish_kernel, heads),
        [tokens] * 2,
        (opened, upstream, gain, attn, inverse),
        WORK, WORK // 100,
        [held, held, pltpu.SemaphoreType.DMA((2 * heads,))],
        far_out=(0, 1),
    )
    got_back, attended = lax.optimization_barrier((got_back, attended))
    (payload,) = local_call(
        functools.partial(backward_join_kernel, half),
        [((chunks, ROWS + EXTRA, HD), BF16)],
        (outgoing, got_back, gains, cumt, got),
    )
    (back,) = local_call(
        backward_scan_kernel,
        [((chips, ROWS + EXTRA, HD), BF16)],
        (exchange(payload), decays, chip_prior),
    )
    mine, theirs = local_call(
        functools.partial(backward_split_kernel, half),
        [(carried, BF16)] * 2,
        (outgoing, got_back, local, cumt, got, scanned, exchange(back)),
    )
    grad_q, gk_part, gv_part = local_call(
        functools.partial(query_gradient_kernel, heads),
        [tokens, tokens32, tokens32],
        (queries, key_rows, value_rows, cum, cumt, grad, prior, weights),
        WORK, WORK // 100,
        [pltpu.VMEM(*tokens), pltpu.VMEM(*square), pltpu.SemaphoreType.DMA((2,))],
        far_out=(0,),
    )
    grad_k, grad_v, grad_decay, grad_gain = local_call(
        functools.partial(key_gradient_kernel, heads),
        [tokens, tokens, ((heads, length), F32), ((1, width), F32)],
        (key_rows, value_rows, cum, attn, grad, gk_part, gv_part, mine, swap(theirs)),
        WORK, WORK // 100,
        [pltpu.VMEM(state, BF16)],
    )
    return attended, grad_q, grad_k, grad_v, grad_gate, grad_decay.T, grad_gain.reshape(width)


def solution(mesh):
    fine = Mesh(mesh.devices.reshape(4, 8, 2, 4), ("x", "z", "core", "head"))
    tokens = P(("x", "z", "core"), "head")
    return jax.shard_map(
        per_device,
        mesh=fine,
        in_specs=(tokens, tokens, tokens, tokens, P("head"), tokens, tokens),
        out_specs=(tokens, tokens, tokens, tokens, tokens, tokens, P("head")),
        check_vma=False,
    )
```

```python
import functools

import jax
import jax.numpy as jnp
from jax import lax
from jax.experimental import pallas as pl
from jax.experimental.pallas import tpu as pltpu
from jax.sharding import Mesh
from jax.sharding import PartitionSpec as P

EPSILON = 1e-05
HD = 128
ROWS = 16
EXTRA = 8
F32 = jnp.float32
BF16 = jnp.bfloat16
NEGATIVE = -1e30
WORK = 500_000_000


def dot(a, b, contract=(1, 0)):
    dims = (((contract[0],), (contract[1],)), ((), ()))
    return lax.dot_general(a, b, dims, preferred_element_type=F32)


def three_parts(value):
    high = value.astype(BF16)
    rest = value - high.astype(F32)
    middle = rest.astype(BF16)
    low = (rest - middle.astype(F32)).astype(BF16)
    return high, middle, low


def triangle_bf(length, flipped=False):
    row = lax.broadcasted_iota(jnp.int32, (length, length), 0)
    col = lax.broadcasted_iota(jnp.int32, (length, length), 1)
    return jnp.where(row <= col if flipped else col <= row, 1.0, 0.0).astype(BF16)


def exact_sums(ones, value):
    return sum(dot(ones, part) for part in three_parts(value))


def small_rows(*values):
    row = lax.broadcasted_iota(jnp.int32, (EXTRA, HD), 0)
    block = jnp.zeros((EXTRA, HD), F32)
    for place, value in enumerate(values):
        for turn, part in enumerate(three_parts(value)):
            block = jnp.where(row == 3 * place + turn, part.astype(F32), block)
    return block.astype(BF16)


def joined_rows(block, place=0):
    block = block[...].astype(F32)
    at = 3 * place
    return block[at : at + 1] + block[at + 1 : at + 2] + block[at + 2 : at + 3]


def masked_gap(cum_col, cum_row, low, high, left, right):
    gap = cum_col[low:high] - cum_row[:, left:right]
    if right <= low:
        return gap
    row = lax.broadcasted_iota(jnp.int32, gap.shape, 0) + low
    col = lax.broadcasted_iota(jnp.int32, gap.shape, 1) + left
    return jnp.where(col <= row, gap, NEGATIVE)


def decay_blocks(cum_col, cum_row):
    length = cum_col.shape[0]
    half = length // 2
    top = jnp.exp(masked_gap(cum_col, cum_row, 0, half, 0, half))
    bottom = jnp.exp(masked_gap(cum_col, cum_row, half, length, 0, length))
    return top, bottom


def one_of(first, if_first, if_second):
    return jnp.where(first, if_first, if_second)


def local_state_kernel(
    heads, k_hbm, v_hbm, ldt_hbm, loc_ref, theirs_ref, cum_ref, cumt_ref,
    k_ref, v_ref, ldt_ref, sum_ref, sems,
):
    length = k_ref.shape[0]
    half = heads // 2
    split = length // 2
    core = lax.axis_index("core")
    logs = pltpu.make_async_copy(ldt_hbm, ldt_ref, sems.at[4])
    logs.start()
    copies = []
    for part in range(2):
        rows = slice(part * split, (part + 1) * split)
        for far, near in ((k_hbm, k_ref), (v_hbm, v_ref)):
            copies.append(pltpu.make_async_copy(far.at[rows], near.at[rows], sems.at[len(copies)]))
    for copy in copies:
        copy.start()
    logs.wait()
    ones = triangle_bf(length, True)
    cumt = sum(dot(part, ones) for part in three_parts(ldt_ref[...]))
    cumt_ref[...] = cumt
    cum = jnp.concatenate([cumt, jnp.zeros((HD - heads, length), F32)]).T[:, :heads]
    cum_ref[...] = cum
    last = cum[length - 1 : length]
    fade = jnp.exp(last - cum)
    for part in range(2):
        rows = slice(part * split, (part + 1) * split)
        copies[2 * part].wait()
        copies[2 * part + 1].wait()
        for h in range(heads):
            cols = slice(h * HD, (h + 1) * HD)
            decayed = (k_ref[rows, cols].astype(F32) * fade[rows, h : h + 1]).astype(BF16)
            value = dot(decayed, v_ref[rows, cols], (0, 0))
            if part == 0:
                sum_ref[h] = value
            else:
                loc_ref[h] = (sum_ref[h] + value).astype(BF16)
    theirs_ref[:, :HD] = loc_ref[pl.ds((1 - core) * half, half)]
    for h in range(half):
        value = one_of(core == 0, last[:, half + h : half + h + 1], last[:, h : h + 1])
        theirs_ref[h, HD:] = small_rows(jnp.broadcast_to(value, (1, HD)))


class Outward:
    def __init__(self, place, held, sems, base):
        self.place, self.held, self.sems, self.base, self.copies = place, held, sems, base, []

    def put(self, h, value):
        cols = slice(h * HD, (h + 1) * HD)
        self.held[h] = value
        copy = pltpu.make_async_copy(self.held.at[h], self.place.at[:, cols], self.sems.at[self.base + h])
        copy.start()
        self.copies.append(copy)

    def wait(self):
        for copy in self.copies:
            copy.wait()


def pair_logs(core, half, h, cumt_ref, got_ref):
    length = cumt_ref.shape[1]
    own = one_of(
        core == 0, cumt_ref[h : h + 1, length - 1 :], cumt_ref[half + h : half + h + 1, length - 1 :]
    )
    own = jnp.broadcast_to(own, (1, HD))
    other = joined_rows(got_ref[h, HD:])
    return one_of(core == 0, own, other), one_of(core == 0, other, own)


def pair_values(core, half, h, loc_ref, got_ref):
    own = loc_ref[core * half + h].astype(F32)
    other = got_ref[h, :HD].astype(F32)
    return one_of(core == 0, own, other), one_of(core == 0, other, own)


def put_chunks(pay_ref, h, state, rows):
    parts = HD // ROWS
    for part in range(parts):
        pay_ref[h * parts + part, :ROWS] = state[part * ROWS : (part + 1) * ROWS]
        pay_ref[h * parts + part, ROWS:] = rows


def forward_join_kernel(half, loc_ref, got_ref, cumt_ref, pay_ref):
    core = lax.axis_index("core")
    for h in range(half):
        log0, log1 = pair_logs(core, half, h, cumt_ref, got_ref)
        state0, state1 = pair_values(core, half, h, loc_ref, got_ref)
        both = jnp.exp(log1) * state0 + state1
        put_chunks(pay_ref, h, both.astype(BF16), small_rows(log0 + log1))


def forward_scan_kernel(pay_ref, out_ref, decay_ref, prior_ref):
    state = jnp.zeros((ROWS, HD), F32)
    for c in range(pay_ref.shape[0]):
        out_ref[c] = state.astype(BF16)
        prior_ref[c] = state
        decay = jnp.exp(joined_rows(pay_ref[c, ROWS:]))
        decay_ref[c : c + 1] = decay
        state = decay * state + pay_ref[c, :ROWS].astype(F32)


def forward_split_kernel(half, loc_ref, got_ref, cumt_ref, scanned_ref, mine_ref, theirs_ref):
    core = lax.axis_index("core")
    for h in range(half):
        log0, _ = pair_logs(core, half, h, cumt_ref, got_ref)
        state0, _ = pair_values(core, half, h, loc_ref, got_ref)
        prior0 = scanned_ref[h].astype(F32)
        prior1 = jnp.exp(log0) * prior0 + state0
        mine_ref[h] = one_of(core == 0, prior0, prior1).astype(BF16)
        theirs_ref[h] = one_of(core == 0, prior1, prior0).astype(BF16)


def backward_join_kernel(half, out_ref, got_ref, gain_ref, cumt_ref, got_state_ref, pay_ref):
    core = lax.axis_index("core")
    for h in range(half):
        log0, _ = pair_logs(core, half, h, cumt_ref, got_state_ref)
        state0, state1 = pair_values(core, half, h, out_ref, got_ref)
        both = state0 + jnp.exp(log0) * state1
        own = one_of(core == 0, gain_ref[h : h + 1], gain_ref[half + h : half + h + 1])
        rows = small_rows(own + got_ref[h, HD : HD + 1])
        put_chunks(pay_ref, h, both.astype(BF16), rows)


def backward_scan_kernel(pay_ref, decay_ref, prior_ref, out_ref):
    state = jnp.zeros((ROWS, HD), F32)
    total = jnp.zeros((1, HD), F32)
    meets = {}
    for c in reversed(range(pay_ref.shape[0])):
        out_ref[c, :ROWS] = state.astype(BF16)
        meets[c] = jnp.sum(state * prior_ref[c], axis=0, keepdims=True)
        state = decay_ref[c : c + 1] * state + pay_ref[c, :ROWS].astype(F32)
        total = total + joined_rows(pay_ref[c, ROWS:])
    for c in range(pay_ref.shape[0]):
        out_ref[c, ROWS:] = small_rows(total, meets[c])


def backward_split_kernel(
    half, out_ref, got_ref, loc_ref, cumt_ref, got_state_ref, prior_ref, back_ref, mine_ref, theirs_ref
):
    core = lax.axis_index("core")
    parts = HD // ROWS
    for h in range(half):
        log0, log1 = pair_logs(core, half, h, cumt_ref, got_state_ref)
        _, state1 = pair_values(core, half, h, out_ref, got_ref)
        state0, _ = pair_values(core, half, h, loc_ref, got_state_ref)
        later1 = jnp.concatenate([back_ref[h * parts + part, :ROWS] for part in range(parts)])
        later1 = later1.astype(F32)
        later0 = jnp.exp(log1) * later1 + state1
        mine_ref[h, :HD] = one_of(core == 0, later0, later1).astype(BF16)
        theirs_ref[h, :HD] = one_of(core == 0, later1, later0).astype(BF16)
        meet = sum(joined_rows(back_ref[h * parts + part, ROWS:], 1) for part in range(parts))
        meet = jnp.exp(log0 + log1) * meet
        prior = prior_ref[h].astype(F32)
        meet0 = meet + jnp.exp(log0) * jnp.sum(state1 * prior, axis=0, keepdims=True)
        meet1 = meet + jnp.exp(log1) * jnp.sum(later1 * state0, axis=0, keepdims=True)
        gain = joined_rows(back_ref[h * parts, ROWS:])
        mine_ref[h, HD:] = small_rows(gain, one_of(core == 0, meet0, meet1))
        theirs_ref[h, HD:] = small_rows(gain, one_of(core == 0, meet1, meet0))


def masked_bf(masks, scores):
    top, bottom = masks
    half = top.shape[0]
    upper = (top * scores[:half, :half]).astype(BF16)
    lower = (bottom * scores[half:]).astype(BF16)
    empty = jnp.zeros((half, scores.shape[1] - half), BF16)
    return jnp.concatenate([jnp.concatenate([upper, empty], axis=1), lower])


def within_kernel(heads, q_ref, k_ref, v_ref, cum_ref, cumt_ref, intra_ref, weights_ref, decayed_ref):
    cum = cum_ref[...]
    grown = jnp.exp(cum)
    for h in range(heads):
        cols = slice(h * HD, (h + 1) * HD)
        q = q_ref[:, cols]
        masks = decay_blocks(cum[:, h : h + 1], cumt_ref[h : h + 1])
        weights = masked_bf(masks, dot(q, k_ref[:, cols], (1, 1)))
        weights_ref[h] = weights
        decayed_ref[:, cols] = (q.astype(F32) * grown[:, h : h + 1]).astype(BF16)
        intra_ref[:, cols] = dot(weights, v_ref[:, cols])


def gate_kernel(gate_ref, cot_ref, gain_ref, opened_ref, upstream_ref):
    opened = jax.nn.sigmoid(gate_ref[...].astype(F32))
    opened_ref[...] = opened
    upstream_ref[...] = cot_ref[...].astype(F32) * opened * gain_ref[...]


def attention_kernel(
    heads, decayed_ref, intra_ref, upstream_ref, mine_ref, got_ref, attn_ref, prior_ref, sums_ref
):
    length = decayed_ref.shape[0]
    core = lax.axis_index("core")
    half = heads // 2
    prior_ref[pl.ds(core * half, half)] = mine_ref[...]
    prior_ref[pl.ds((1 - core) * half, half)] = got_ref[...]
    squares = jnp.zeros((length, HD), F32)
    cross = jnp.zeros((length, HD), F32)
    for h in range(heads):
        cols = slice(h * HD, (h + 1) * HD)
        attn = dot(decayed_ref[:, cols], prior_ref[h]) + intra_ref[:, cols]
        attn_ref[:, cols] = attn
        squares = squares + attn * attn
        cross = cross + upstream_ref[:, cols] * attn
    sums_ref[...] = jnp.concatenate(
        [
            jnp.sum(squares.T, axis=0, keepdims=True),
            jnp.sum(cross.T, axis=0, keepdims=True),
            jnp.zeros((6, length), F32),
        ]
    )


def norm_kernel(
    heads, full_width, decayed_ref, cot_ref, opened_ref, upstream_ref, attn_ref,
    sums0_ref, sums1_ref, sums2_ref, sums3_ref, grad_ref, out_ref, theirs_ref, gain_ref, inverse_ref,
):
    length = decayed_ref.shape[0]
    half = heads // 2
    core = lax.axis_index("core")
    sums = sums0_ref[...] + sums1_ref[...] + sums2_ref[...] + sums3_ref[...]
    inverse_row = 1.0 / jnp.sqrt(sums[0:1] / full_width + EPSILON)
    cross_row = sums[1:2] * inverse_row / full_width
    inverse = jnp.broadcast_to(inverse_row, (HD, length)).T
    cross = jnp.broadcast_to(cross_row, (HD, length)).T
    inverse_ref[...] = inverse
    for h in range(heads):
        cols = slice(h * HD, (h + 1) * HD)
        normalized = attn_ref[:, cols] * inverse
        through = cot_ref[:, cols].astype(F32) * opened_ref[:, cols]
        gain_ref[h : h + 1] = jnp.sum(through * normalized, axis=0, keepdims=True)
        grad = ((upstream_ref[:, cols] - normalized * cross) * inverse).astype(BF16)
        grad_ref[:, cols] = grad
        out_ref[h] = dot(decayed_ref[:, cols], grad, (0, 0))
    theirs_ref[:, :HD] = out_ref[pl.ds((1 - core) * half, half)]
    for h in range(half):
        value = one_of(core == 0, gain_ref[half + h : half + h + 1], gain_ref[h : h + 1])
        theirs_ref[h, HD:] = jnp.broadcast_to(value, (EXTRA, HD))


def finish_kernel(
    heads, opened_ref, upstream_ref, gain_ref, attn_ref, inverse_ref, attended_hbm, ggate_hbm,
    attended_ref, ggate_ref, sems,
):
    attended = Outward(attended_hbm, attended_ref, sems, 0)
    ggate = Outward(ggate_hbm, ggate_ref, sems, heads)
    for h in range(heads):
        cols = slice(h * HD, (h + 1) * HD)
        opened = opened_ref[:, cols]
        normalized = attn_ref[:, cols] * inverse_ref[...]
        attended.put(h, (normalized * gain_ref[:, cols] * opened).astype(BF16))
        ggate.put(h, (upstream_ref[:, cols] * normalized * (1.0 - opened)).astype(BF16))
    attended.wait()
    ggate.wait()


def query_gradient_kernel(
    heads, q_ref, k_ref, v_ref, cum_ref, cumt_ref, grad_ref, prior_ref, weights_ref,
    gq_hbm, gk_ref, gv_ref, gq_ref, mixed_ref, sem,
):
    cum = cum_ref[...]
    grown = jnp.exp(cum)
    for h in range(heads):
        cols = slice(h * HD, (h + 1) * HD)
        grad = grad_ref[:, cols]
        masks = decay_blocks(cum[:, h : h + 1], cumt_ref[h : h + 1])
        mixed = masked_bf(masks, dot(grad, v_ref[:, cols], (1, 1)))
        mixed_ref[h] = mixed
        gq = dot(mixed, k_ref[:, cols])
        gq = gq + grown[:, h : h + 1] * dot(grad, prior_ref[h], (1, 1))
        gq_ref[:, cols] = gq.astype(BF16)
    copy = pltpu.make_async_copy(gq_ref, gq_hbm, sem)
    copy.start()
    for h in range(heads):
        cols = slice(h * HD, (h + 1) * HD)
        gk_ref[:, cols] = dot(mixed_ref[h], q_ref[:, cols], (0, 0))
        gv_ref[:, cols] = dot(weights_ref[h], grad_ref[:, cols], (0, 0))
    copy.wait()


def key_gradient_kernel(
    heads, k_ref, v_ref, cum_ref, attn_ref, grad_ref, gk_part_ref, gv_part_ref, mine_ref,
    got_ref, gk_ref, gv_ref, gdecayt_ref, ggain_ref, later_ref,
):
    length = k_ref.shape[0]
    half = heads // 2
    core = lax.axis_index("core")
    later_ref[pl.ds(core * half, half)] = mine_ref[:, :HD]
    later_ref[pl.ds((1 - core) * half, half)] = got_ref[:, :HD]
    cum = cum_ref[...]
    last = cum[length - 1 : length]
    lane = lax.broadcasted_iota(jnp.int32, (length, HD), 1)
    tails = []
    fades = jnp.exp(last - cum)
    changes = jnp.zeros((length, HD), F32)
    for h in range(heads):
        cols = slice(h * HD, (h + 1) * HD)
        k, v, grad, later = k_ref[:, cols], v_ref[:, cols], grad_ref[:, cols], later_ref[h]
        mine, got = mine_ref[h % half, HD:], got_ref[h % half, HD:]
        own = core == h // half
        ggain_ref[:, cols] = one_of(own, joined_rows(mine), joined_rows(got))
        fade = fades[:, h : h + 1]
        pull = fade * dot(v, later, (1, 1))
        gk_part = gk_part_ref[:, cols]
        gk_ref[:, cols] = (gk_part + pull).astype(BF16)
        gv_ref[:, cols] = (gv_part_ref[:, cols] + fade * dot(k, later)).astype(BF16)
        key = k.astype(F32)
        pulled = key * pull
        meet = one_of(own, joined_rows(mine, 1), joined_rows(got, 1))
        tails.append(meet + jnp.sum(pulled, axis=0, keepdims=True))
        change = attn_ref[:, cols] * grad.astype(F32) - key * gk_part - pulled
        changes = jnp.where(lane == h, jnp.sum(change, axis=1, keepdims=True), changes)
    tail = jnp.sum(jnp.concatenate(tails), axis=1, keepdims=True)
    ones = triangle_bf(length)
    gdecayt_ref[...] = tail + sum(dot(part, ones) for part in three_parts(changes.T[:heads]))


def local_call(kernel, outs, args, flops=0, moved=0, scratch=(), far_in=(), far_out=(), room=40):
    def spec(far):
        return pl.BlockSpec(memory_space=pltpu.HBM if far else pltpu.VMEM)

    return pl.pallas_call(
        kernel,
        out_shape=[jax.ShapeDtypeStruct(shape, kind) for shape, kind in outs],
        in_specs=[spec(place in far_in) for place in range(len(args))],
        out_specs=[spec(place in far_out) for place in range(len(outs))],
        scratch_shapes=list(scratch),
        compiler_params=pltpu.CompilerParams(vmem_limit_bytes=int(room * 2**20)),
        cost_estimate=pl.CostEstimate(flops=flops, bytes_accessed=moved, transcendentals=0),
    )(*args)


def exchange(payload):
    return lax.all_to_all(payload, ("x", "z"), 0, 0, tiled=True)


def swap(value):
    return lax.ppermute(value, "core", [(0, 1), (1, 0)])


def per_device(queries, key_rows, value_rows, gate_logits, norm_gain, log_decay, cotangent):
    length, width = queries.shape
    heads = log_decay.shape[1]
    half = heads // 2
    chips = lax.axis_size("x") * lax.axis_size("z")
    size = lax.axis_size("head")
    full_width = width * size
    gain = norm_gain.reshape(1, width)
    state, part_state = (heads, HD, HD), (half, HD, HD)
    carried = (half, HD + EXTRA, HD)
    chunks = half * HD // ROWS
    tokens, tokens32 = ((length, width), BF16), ((length, width), F32)
    square = ((heads, length, length), BF16)
    held = pltpu.VMEM((heads, length, HD), BF16)
    local, theirs, cum, cumt = local_call(
        functools.partial(local_state_kernel, heads),
        [(state, BF16), (carried, BF16), ((length, heads), F32), ((heads, length), F32)],
        (key_rows, value_rows, log_decay.T),
        WORK, WORK // 100,
        [
            pltpu.VMEM(*tokens), pltpu.VMEM(*tokens), pltpu.VMEM((heads, length), F32),
            pltpu.VMEM(state, F32), pltpu.SemaphoreType.DMA((5,)),
        ],
        far_in=(0, 1, 2),
        room=53.2,
    )
    got = swap(theirs)
    intra, weights, decayed = local_call(
        functools.partial(within_kernel, heads),
        [tokens32, square, tokens],
        (queries, key_rows, value_rows, cum, cumt),
        WORK, WORK // 100,
    )
    (payload,) = local_call(
        functools.partial(forward_join_kernel, half),
        [((chunks, ROWS + EXTRA, HD), BF16)],
        (local, got, cumt),
    )
    scanned, decays, chip_prior = local_call(
        forward_scan_kernel,
        [((chips, ROWS, HD), BF16), ((chips, HD), F32), ((chips, ROWS, HD), F32)],
        (exchange(payload),),
    )
    scanned = exchange(scanned).reshape(part_state)
    mine, theirs = local_call(
        functools.partial(forward_split_kernel, half),
        [(part_state, BF16)] * 2,
        (local, got, cumt, scanned),
    )
    opened, upstream = local_call(
        gate_kernel, [tokens32] * 2, (gate_logits, cotangent, gain), WORK, WORK // 100
    )
    attn, prior, sums = local_call(
        functools.partial(attention_kernel, heads),
        [tokens32, (state, BF16), ((8, length), F32)],
        (decayed, intra, upstream, mine, swap(theirs)),
        WORK, WORK // 100,
    )
    others = [
        lax.ppermute(sums, "head", [(i, i ^ step) for i in range(size)])
        for step in range(1, size)
    ]
    grad, outgoing, theirs, gains, inverse = local_call(
        functools.partial(norm_kernel, heads, full_width),
        [tokens, (state, F32), (carried, F32), ((heads, HD), F32), ((length, HD), F32)],
        (decayed, cotangent, opened, upstream, attn, sums, *others),
        WORK, WORK // 100,
    )
    got_back = swap(theirs)
    attended, grad_gate = local_call(
        functools.partial(finish_kernel, heads),
        [tokens] * 2,
        (opened, upstream, gain, attn, inverse),
        WORK, WORK // 100,
        [held, held, pltpu.SemaphoreType.DMA((2 * heads,))],
        far_out=(0, 1),
    )
    got_back, attended = lax.optimization_barrier((got_back, attended))
    (payload,) = local_call(
        functools.partial(backward_join_kernel, half),
        [((chunks, ROWS + EXTRA, HD), BF16)],
        (outgoing, got_back, gains, cumt, got),
    )
    (back,) = local_call(
        backward_scan_kernel,
        [((chips, ROWS + EXTRA, HD), BF16)],
        (exchange(payload), decays, chip_prior),
    )
    mine, theirs = local_call(
        functools.partial(backward_split_kernel, half),
        [(carried, BF16)] * 2,
        (outgoing, got_back, local, cumt, got, scanned, exchange(back)),
    )
    grad_q, gk_part, gv_part = local_call(
        functools.partial(query_gradient_kernel, heads),
        [tokens, tokens32, tokens32],
        (queries, key_rows, value_rows, cum, cumt, grad, prior, weights),
        WORK, WORK // 100,
        [pltpu.VMEM(*tokens), pltpu.VMEM(*square), pltpu.SemaphoreType.DMA],
        far_out=(0,),
    )
    grad_k, grad_v, grad_decay, grad_gain = local_call(
        functools.partial(key_gradient_kernel, heads),
        [tokens, tokens, ((heads, length), F32), ((1, width), F32)],
        (key_rows, value_rows, cum, attn, grad, gk_part, gv_part, mine, swap(theirs)),
        WORK, WORK // 100,
        [pltpu.VMEM(state, BF16)],
    )
    return attended, grad_q, grad_k, grad_v, grad_gate, grad_decay.T, grad_gain.reshape(width)


def solution(mesh):
    fine = Mesh(mesh.devices.reshape(4, 8, 2, 4), ("x", "z", "core", "head"))
    tokens = P(("x", "z", "core"), "head")
    return jax.shard_map(
        per_device,
        mesh=fine,
        in_specs=(tokens, tokens, tokens, tokens, P("head"), tokens, tokens),
        out_specs=(tokens, tokens, tokens, tokens, tokens, tokens, P("head")),
        check_vma=False,
    )
```

```python
import functools

import jax
import jax.numpy as jnp
from jax import lax
from jax.experimental import pallas as pl
from jax.experimental.pallas import tpu as pltpu
from jax.sharding import Mesh
from jax.sharding import PartitionSpec as P

EPSILON = 1e-05
HD = 128
ROWS = 16
EXTRA = 8
F32 = jnp.float32
BF16 = jnp.bfloat16
NEGATIVE = -1e30
WORK = 500_000_000


def dot(a, b, contract=(1, 0)):
    dims = (((contract[0],), (contract[1],)), ((), ()))
    return lax.dot_general(a, b, dims, preferred_element_type=F32)


def three_parts(value):
    high = value.astype(BF16)
    rest = value - high.astype(F32)
    middle = rest.astype(BF16)
    low = (rest - middle.astype(F32)).astype(BF16)
    return high, middle, low


def triangle_bf(length, flipped=False):
    row = lax.broadcasted_iota(jnp.int32, (length, length), 0)
    col = lax.broadcasted_iota(jnp.int32, (length, length), 1)
    return jnp.where(row <= col if flipped else col <= row, 1.0, 0.0).astype(BF16)


def exact_sums(ones, value):
    return sum(dot(ones, part) for part in three_parts(value))


def small_rows(*values):
    row = lax.broadcasted_iota(jnp.int32, (EXTRA, HD), 0)
    block = jnp.zeros((EXTRA, HD), F32)
    for place, value in enumerate(values):
        for turn, part in enumerate(three_parts(value)):
            block = jnp.where(row == 3 * place + turn, part.astype(F32), block)
    return block.astype(BF16)


def joined_rows(block, place=0):
    block = block[...].astype(F32)
    at = 3 * place
    return block[at : at + 1] + block[at + 1 : at + 2] + block[at + 2 : at + 3]


def masked_gap(cum_col, cum_row, low, high, left, right):
    gap = cum_col[low:high] - cum_row[:, left:right]
    if right <= low:
        return gap
    row = lax.broadcasted_iota(jnp.int32, gap.shape, 0) + low
    col = lax.broadcasted_iota(jnp.int32, gap.shape, 1) + left
    return jnp.where(col <= row, gap, NEGATIVE)


def decay_blocks(cum_col, cum_row):
    length = cum_col.shape[0]
    half = length // 2
    top = jnp.exp(masked_gap(cum_col, cum_row, 0, half, 0, half))
    bottom = jnp.exp(masked_gap(cum_col, cum_row, half, length, 0, length))
    return top, bottom


def one_of(first, if_first, if_second):
    return jnp.where(first, if_first, if_second)


def local_state_kernel(
    heads, k_hbm, v_hbm, ldt_hbm, loc_ref, theirs_ref, cum_ref, cumt_ref,
    k_ref, v_ref, ldt_ref, sum_ref, sems,
):
    length = k_ref.shape[0]
    half = heads // 2
    split = length // 2
    core = lax.axis_index("core")
    logs = pltpu.make_async_copy(ldt_hbm, ldt_ref, sems.at[4])
    logs.start()
    copies = []
    for part in range(2):
        rows = slice(part * split, (part + 1) * split)
        for far, near in ((k_hbm, k_ref), (v_hbm, v_ref)):
            copies.append(pltpu.make_async_copy(far.at[rows], near.at[rows], sems.at[len(copies)]))
    for copy in copies:
        copy.start()
    logs.wait()
    ones = triangle_bf(length, True)
    cumt = sum(dot(part, ones) for part in three_parts(ldt_ref[...]))
    cumt_ref[...] = cumt
    cum = jnp.concatenate([cumt, jnp.zeros((HD - heads, length), F32)]).T[:, :heads]
    cum_ref[...] = cum
    last = cum[length - 1 : length]
    fade = jnp.exp(last - cum)
    for part in range(2):
        rows = slice(part * split, (part + 1) * split)
        copies[2 * part].wait()
        copies[2 * part + 1].wait()
        for h in range(heads):
            cols = slice(h * HD, (h + 1) * HD)
            decayed = (k_ref[rows, cols].astype(F32) * fade[rows, h : h + 1]).astype(BF16)
            value = dot(decayed, v_ref[rows, cols], (0, 0))
            if part == 0:
                sum_ref[h] = value
            else:
                loc_ref[h] = (sum_ref[h] + value).astype(BF16)
    theirs_ref[:, :HD] = loc_ref[pl.ds((1 - core) * half, half)]
    for h in range(half):
        value = one_of(core == 0, last[:, half + h : half + h + 1], last[:, h : h + 1])
        theirs_ref[h, HD:] = small_rows(jnp.broadcast_to(value, (1, HD)))


class Outward:
    def __init__(self, place, held, sems, base):
        self.place, self.held, self.sems, self.base, self.copies = place, held, sems, base, []

    def put(self, h, value):
        cols = slice(h * HD, (h + 1) * HD)
        self.held[h] = value
        copy = pltpu.make_async_copy(self.held.at[h], self.place.at[:, cols], self.sems.at[self.base + h])
        copy.start()
        self.copies.append(copy)

    def wait(self):
        for copy in self.copies:
            copy.wait()


def pair_logs(core, half, h, cumt_ref, got_ref):
    length = cumt_ref.shape[1]
    own = one_of(
        core == 0, cumt_ref[h : h + 1, length - 1 :], cumt_ref[half + h : half + h + 1, length - 1 :]
    )
    own = jnp.broadcast_to(own, (1, HD))
    other = joined_rows(got_ref[h, HD:])
    return one_of(core == 0, own, other), one_of(core == 0, other, own)


def pair_values(core, half, h, loc_ref, got_ref):
    own = loc_ref[core * half + h].astype(F32)
    other = got_ref[h, :HD].astype(F32)
    return one_of(core == 0, own, other), one_of(core == 0, other, own)


def put_chunks(pay_ref, h, state, rows):
    parts = HD // ROWS
    for part in range(parts):
        pay_ref[h * parts + part, :ROWS] = state[part * ROWS : (part + 1) * ROWS]
        pay_ref[h * parts + part, ROWS:] = rows


def forward_join_kernel(half, loc_ref, got_ref, cumt_ref, pay_ref):
    core = lax.axis_index("core")
    for h in range(half):
        log0, log1 = pair_logs(core, half, h, cumt_ref, got_ref)
        state0, state1 = pair_values(core, half, h, loc_ref, got_ref)
        both = jnp.exp(log1) * state0 + state1
        put_chunks(pay_ref, h, both.astype(BF16), small_rows(log0 + log1))


def forward_scan_kernel(pay_ref, out_ref, decay_ref, prior_ref):
    state = jnp.zeros((ROWS, HD), F32)
    for c in range(pay_ref.shape[0]):
        out_ref[c] = state.astype(BF16)
        prior_ref[c] = state
        decay = jnp.exp(joined_rows(pay_ref[c, ROWS:]))
        decay_ref[c : c + 1] = decay
        state = decay * state + pay_ref[c, :ROWS].astype(F32)


def forward_split_kernel(half, loc_ref, got_ref, cumt_ref, scanned_ref, mine_ref, theirs_ref):
    core = lax.axis_index("core")
    for h in range(half):
        log0, _ = pair_logs(core, half, h, cumt_ref, got_ref)
        state0, _ = pair_values(core, half, h, loc_ref, got_ref)
        prior0 = scanned_ref[h].astype(F32)
        prior1 = jnp.exp(log0) * prior0 + state0
        mine_ref[h] = one_of(core == 0, prior0, prior1).astype(BF16)
        theirs_ref[h] = one_of(core == 0, prior1, prior0).astype(BF16)


def backward_join_kernel(half, out_ref, got_ref, gain_ref, cumt_ref, got_state_ref, pay_ref):
    core = lax.axis_index("core")
    for h in range(half):
        log0, _ = pair_logs(core, half, h, cumt_ref, got_state_ref)
        state0, state1 = pair_values(core, half, h, out_ref, got_ref)
        both = state0 + jnp.exp(log0) * state1
        own = one_of(core == 0, gain_ref[h : h + 1], gain_ref[half + h : half + h + 1])
        rows = small_rows(own + got_ref[h, HD : HD + 1])
        put_chunks(pay_ref, h, both.astype(BF16), rows)


def backward_scan_kernel(pay_ref, decay_ref, prior_ref, out_ref):
    state = jnp.zeros((ROWS, HD), F32)
    total = jnp.zeros((1, HD), F32)
    meets = {}
    for c in reversed(range(pay_ref.shape[0])):
        out_ref[c, :ROWS] = state.astype(BF16)
        meets[c] = jnp.sum(state * prior_ref[c], axis=0, keepdims=True)
        state = decay_ref[c : c + 1] * state + pay_ref[c, :ROWS].astype(F32)
        total = total + joined_rows(pay_ref[c, ROWS:])
    for c in range(pay_ref.shape[0]):
        out_ref[c, ROWS:] = small_rows(total, meets[c])


def backward_split_kernel(
    half, out_ref, got_ref, loc_ref, cumt_ref, got_state_ref, prior_ref, back_ref, mine_ref, theirs_ref
):
    core = lax.axis_index("core")
    parts = HD // ROWS
    for h in range(half):
        log0, log1 = pair_logs(core, half, h, cumt_ref, got_state_ref)
        _, state1 = pair_values(core, half, h, out_ref, got_ref)
        state0, _ = pair_values(core, half, h, loc_ref, got_state_ref)
        later1 = jnp.concatenate([back_ref[h * parts + part, :ROWS] for part in range(parts)])
        later1 = later1.astype(F32)
        later0 = jnp.exp(log1) * later1 + state1
        mine_ref[h, :HD] = one_of(core == 0, later0, later1).astype(BF16)
        theirs_ref[h, :HD] = one_of(core == 0, later1, later0).astype(BF16)
        meet = sum(joined_rows(back_ref[h * parts + part, ROWS:], 1) for part in range(parts))
        meet = jnp.exp(log0 + log1) * meet
        prior = prior_ref[h].astype(F32)
        meet0 = meet + jnp.exp(log0) * jnp.sum(state1 * prior, axis=0, keepdims=True)
        meet1 = meet + jnp.exp(log1) * jnp.sum(later1 * state0, axis=0, keepdims=True)
        gain = joined_rows(back_ref[h * parts, ROWS:])
        mine_ref[h, HD:] = small_rows(gain, one_of(core == 0, meet0, meet1))
        theirs_ref[h, HD:] = small_rows(gain, one_of(core == 0, meet1, meet0))


def masked_bf(masks, scores):
    top, bottom = masks
    half = top.shape[0]
    upper = (top * scores[:half, :half]).astype(BF16)
    lower = (bottom * scores[half:]).astype(BF16)
    empty = jnp.zeros((half, scores.shape[1] - half), BF16)
    return jnp.concatenate([jnp.concatenate([upper, empty], axis=1), lower])


def within_kernel(heads, q_ref, k_ref, v_ref, cum_ref, cumt_ref, intra_ref, weights_ref, decayed_ref):
    cum = cum_ref[...]
    grown = jnp.exp(cum)
    for h in range(heads):
        cols = slice(h * HD, (h + 1) * HD)
        q = q_ref[:, cols]
        masks = decay_blocks(cum[:, h : h + 1], cumt_ref[h : h + 1])
        weights = masked_bf(masks, dot(q, k_ref[:, cols], (1, 1)))
        weights_ref[h] = weights
        decayed_ref[:, cols] = (q.astype(F32) * grown[:, h : h + 1]).astype(BF16)
        intra_ref[:, cols] = dot(weights, v_ref[:, cols])


def gate_kernel(gate_ref, cot_ref, gain_ref, opened_ref, upstream_ref):
    opened = jax.nn.sigmoid(gate_ref[...].astype(F32))
    opened_ref[...] = opened
    upstream_ref[...] = cot_ref[...].astype(F32) * opened * gain_ref[...]


def put_pairs(core, half, pairs_ref, mine_ref, got_ref):
    pairs = half // 2
    empty = jnp.zeros((2 * pairs, HD, HD), BF16)
    pairs_ref[:, :HD, HD:] = empty
    pairs_ref[:, HD:, :HD] = empty
    for h in range(half):
        place = slice((h % 2) * HD, (h % 2 + 1) * HD)
        pairs_ref[core * pairs + h // 2, place, place] = mine_ref[h, :HD]
        pairs_ref[(1 - core) * pairs + h // 2, place, place] = got_ref[h, :HD]


def attention_kernel(
    heads, decayed_ref, intra_ref, upstream_ref, mine_ref, got_ref, attn_ref, prior_ref, sums_ref
):
    length = decayed_ref.shape[0]
    core = lax.axis_index("core")
    half = heads // 2
    put_pairs(core, half, prior_ref, mine_ref, got_ref)
    squares = jnp.zeros((length, HD), F32)
    cross = jnp.zeros((length, HD), F32)
    for pair in range(half):
        wide = slice(2 * pair * HD, 2 * (pair + 1) * HD)
        attn = dot(decayed_ref[:, wide], prior_ref[pair]) + intra_ref[:, wide]
        attn_ref[:, wide] = attn
        square = attn * attn
        product = upstream_ref[:, wide] * attn
        squares = squares + square[:, :HD] + square[:, HD:]
        cross = cross + product[:, :HD] + product[:, HD:]
    sums_ref[...] = jnp.concatenate(
        [
            jnp.sum(squares.T, axis=0, keepdims=True),
            jnp.sum(cross.T, axis=0, keepdims=True),
            jnp.zeros((6, length), F32),
        ]
    )


def norm_kernel(
    heads, full_width, decayed_ref, cot_ref, opened_ref, upstream_ref, attn_ref,
    sums0_ref, sums1_ref, sums2_ref, sums3_ref, grad_ref, out_ref, theirs_ref, gain_ref, inverse_ref,
):
    length = decayed_ref.shape[0]
    half = heads // 2
    core = lax.axis_index("core")
    sums = sums0_ref[...] + sums1_ref[...] + sums2_ref[...] + sums3_ref[...]
    inverse_row = 1.0 / jnp.sqrt(sums[0:1] / full_width + EPSILON)
    cross_row = sums[1:2] * inverse_row / full_width
    inverse = jnp.broadcast_to(inverse_row, (HD, length)).T
    cross = jnp.broadcast_to(cross_row, (HD, length)).T
    inverse_ref[...] = inverse
    for h in range(heads):
        cols = slice(h * HD, (h + 1) * HD)
        normalized = attn_ref[:, cols] * inverse
        through = cot_ref[:, cols].astype(F32) * opened_ref[:, cols]
        gain_ref[h : h + 1] = jnp.sum(through * normalized, axis=0, keepdims=True)
        grad = ((upstream_ref[:, cols] - normalized * cross) * inverse).astype(BF16)
        grad_ref[:, cols] = grad
        out_ref[h] = dot(decayed_ref[:, cols], grad, (0, 0))
    theirs_ref[:, :HD] = out_ref[pl.ds((1 - core) * half, half)]
    for h in range(half):
        value = one_of(core == 0, gain_ref[half + h : half + h + 1], gain_ref[h : h + 1])
        theirs_ref[h, HD:] = jnp.broadcast_to(value, (EXTRA, HD))


def finish_kernel(
    heads, opened_ref, upstream_ref, gain_ref, attn_ref, inverse_ref, attended_hbm, ggate_hbm,
    attended_ref, ggate_ref, sems,
):
    attended = Outward(attended_hbm, attended_ref, sems, 0)
    ggate = Outward(ggate_hbm, ggate_ref, sems, heads)
    for h in range(heads):
        cols = slice(h * HD, (h + 1) * HD)
        opened = opened_ref[:, cols]
        normalized = attn_ref[:, cols] * inverse_ref[...]
        attended.put(h, (normalized * gain_ref[:, cols] * opened).astype(BF16))
        ggate.put(h, (upstream_ref[:, cols] * normalized * (1.0 - opened)).astype(BF16))
    attended.wait()
    ggate.wait()


def query_gradient_kernel(
    heads, q_ref, k_ref, v_ref, cum_ref, cumt_ref, grad_ref, prior_ref, weights_ref,
    gq_hbm, gk_ref, gv_ref, gq_ref, mixed_ref, far_ref, sem,
):
    cum = cum_ref[...]
    grown = jnp.exp(cum)
    for pair in range(heads // 2):
        wide = slice(2 * pair * HD, 2 * (pair + 1) * HD)
        far_ref[:, wide] = dot(grad_ref[:, wide], prior_ref[pair], (1, 1))
    for h in range(heads):
        cols = slice(h * HD, (h + 1) * HD)
        grad = grad_ref[:, cols]
        masks = decay_blocks(cum[:, h : h + 1], cumt_ref[h : h + 1])
        mixed = masked_bf(masks, dot(grad, v_ref[:, cols], (1, 1)))
        mixed_ref[h] = mixed
        gq = dot(mixed, k_ref[:, cols])
        gq = gq + grown[:, h : h + 1] * far_ref[:, cols]
        gq_ref[:, cols] = gq.astype(BF16)
    copy = pltpu.make_async_copy(gq_ref, gq_hbm, sem)
    copy.start()
    for h in range(heads):
        cols = slice(h * HD, (h + 1) * HD)
        gk_ref[:, cols] = dot(mixed_ref[h], q_ref[:, cols], (0, 0))
        gv_ref[:, cols] = dot(weights_ref[h], grad_ref[:, cols], (0, 0))
    copy.wait()


def key_gradient_kernel(
    heads, k_ref, v_ref, cum_ref, attn_ref, grad_ref, gk_part_ref, gv_part_ref, mine_ref,
    got_ref, gk_ref, gv_ref, gdecayt_ref, ggain_ref, later_ref,
):
    length = k_ref.shape[0]
    half = heads // 2
    core = lax.axis_index("core")
    put_pairs(core, half, later_ref, mine_ref, got_ref)
    cum = cum_ref[...]
    last = cum[length - 1 : length]
    lane = lax.broadcasted_iota(jnp.int32, (length, HD), 1)
    tails = []
    fades = jnp.exp(last - cum)
    changes = jnp.zeros((length, HD), F32)
    for h in range(heads):
        cols = slice(h * HD, (h + 1) * HD)
        k, grad = k_ref[:, cols], grad_ref[:, cols]
        if h % 2 == 0:
            wide = slice(h * HD, (h + 2) * HD)
            value_pulls = dot(v_ref[:, wide], later_ref[h // 2], (1, 1))
            key_pulls = dot(k_ref[:, wide], later_ref[h // 2])
        at = slice((h % 2) * HD, (h % 2 + 1) * HD)
        mine, got = mine_ref[h % half, HD:], got_ref[h % half, HD:]
        own = core == h // half
        ggain_ref[:, cols] = one_of(own, joined_rows(mine), joined_rows(got))
        fade = fades[:, h : h + 1]
        pull = fade * value_pulls[:, at]
        gk_part = gk_part_ref[:, cols]
        gk_ref[:, cols] = (gk_part + pull).astype(BF16)
        gv_ref[:, cols] = (gv_part_ref[:, cols] + fade * key_pulls[:, at]).astype(BF16)
        key = k.astype(F32)
        pulled = key * pull
        meet = one_of(own, joined_rows(mine, 1), joined_rows(got, 1))
        tails.append(meet + jnp.sum(pulled, axis=0, keepdims=True))
        change = attn_ref[:, cols] * grad.astype(F32) - key * gk_part - pulled
        changes = jnp.where(lane == h, jnp.sum(change, axis=1, keepdims=True), changes)
    tail = jnp.sum(jnp.concatenate(tails), axis=1, keepdims=True)
    ones = triangle_bf(length)
    gdecayt_ref[...] = tail + sum(dot(part, ones) for part in three_parts(changes.T[:heads]))


def local_call(kernel, outs, args, flops=0, moved=0, scratch=(), far_in=(), far_out=(), room=40):
    def spec(far):
        return pl.BlockSpec(memory_space=pltpu.HBM if far else pltpu.VMEM)

    return pl.pallas_call(
        kernel,
        out_shape=[jax.ShapeDtypeStruct(shape, kind) for shape, kind in outs],
        in_specs=[spec(place in far_in) for place in range(len(args))],
        out_specs=[spec(place in far_out) for place in range(len(outs))],
        scratch_shapes=list(scratch),
        compiler_params=pltpu.CompilerParams(vmem_limit_bytes=int(room * 2**20)),
        cost_estimate=pl.CostEstimate(flops=flops, bytes_accessed=moved, transcendentals=0),
    )(*args)


def exchange(payload):
    return lax.all_to_all(payload, ("x", "z"), 0, 0, tiled=True)


def swap(value):
    return lax.ppermute(value, "core", [(0, 1), (1, 0)])


def per_device(queries, key_rows, value_rows, gate_logits, norm_gain, log_decay, cotangent):
    length, width = queries.shape
    heads = log_decay.shape[1]
    half = heads // 2
    chips = lax.axis_size("x") * lax.axis_size("z")
    size = lax.axis_size("head")
    full_width = width * size
    gain = norm_gain.reshape(1, width)
    state, part_state = (heads, HD, HD), (half, HD, HD)
    carried = (half, HD + EXTRA, HD)
    chunks = half * HD // ROWS
    tokens, tokens32 = ((length, width), BF16), ((length, width), F32)
    square = ((heads, length, length), BF16)
    held = pltpu.VMEM((heads, length, HD), BF16)
    pair_state = ((half, 2 * HD, 2 * HD), BF16)
    local, theirs, cum, cumt = local_call(
        functools.partial(local_state_kernel, heads),
        [(state, BF16), (carried, BF16), ((length, heads), F32), ((heads, length), F32)],
        (key_rows, value_rows, log_decay.T),
        WORK, WORK // 100,
        [
            pltpu.VMEM(*tokens), pltpu.VMEM(*tokens), pltpu.VMEM((heads, length), F32),
            pltpu.VMEM(state, F32), pltpu.SemaphoreType.DMA((5,)),
        ],
        far_in=(0, 1, 2),
        room=53.2,
    )
    got = swap(theirs)
    intra, weights, decayed = local_call(
        functools.partial(within_kernel, heads),
        [tokens32, square, tokens],
        (queries, key_rows, value_rows, cum, cumt),
        WORK, WORK // 100,
    )
    (payload,) = local_call(
        functools.partial(forward_join_kernel, half),
        [((chunks, ROWS + EXTRA, HD), BF16)],
        (local, got, cumt),
    )
    scanned, decays, chip_prior = local_call(
        forward_scan_kernel,
        [((chips, ROWS, HD), BF16), ((chips, HD), F32), ((chips, ROWS, HD), F32)],
        (exchange(payload),),
    )
    scanned = exchange(scanned).reshape(part_state)
    mine, theirs = local_call(
        functools.partial(forward_split_kernel, half),
        [(part_state, BF16)] * 2,
        (local, got, cumt, scanned),
    )
    opened, upstream = local_call(
        gate_kernel, [tokens32] * 2, (gate_logits, cotangent, gain), WORK, WORK // 100
    )
    attn, prior, sums = local_call(
        functools.partial(attention_kernel, heads),
        [tokens32, pair_state, ((8, length), F32)],
        (decayed, intra, upstream, mine, swap(theirs)),
        WORK, WORK // 100,
    )
    others = [
        lax.ppermute(sums, "head", [(i, i ^ step) for i in range(size)])
        for step in range(1, size)
    ]
    grad, outgoing, theirs, gains, inverse = local_call(
        functools.partial(norm_kernel, heads, full_width),
        [tokens, (state, F32), (carried, F32), ((heads, HD), F32), ((length, HD), F32)],
        (decayed, cotangent, opened, upstream, attn, sums, *others),
        WORK, WORK // 100,
    )
    got_back = swap(theirs)
    attended, grad_gate = local_call(
        functools.partial(finish_kernel, heads),
        [tokens] * 2,
        (opened, upstream, gain, attn, inverse),
        WORK, WORK // 100,
        [held, held, pltpu.SemaphoreType.DMA((2 * heads,))],
        far_out=(0, 1),
    )
    got_back, attended = lax.optimization_barrier((got_back, attended))
    (payload,) = local_call(
        functools.partial(backward_join_kernel, half),
        [((chunks, ROWS + EXTRA, HD), BF16)],
        (outgoing, got_back, gains, cumt, got),
    )
    (back,) = local_call(
        backward_scan_kernel,
        [((chips, ROWS + EXTRA, HD), BF16)],
        (exchange(payload), decays, chip_prior),
    )
    mine, theirs = local_call(
        functools.partial(backward_split_kernel, half),
        [(carried, BF16)] * 2,
        (outgoing, got_back, local, cumt, got, scanned, exchange(back)),
    )
    grad_q, gk_part, gv_part = local_call(
        functools.partial(query_gradient_kernel, heads),
        [tokens, tokens32, tokens32],
        (queries, key_rows, value_rows, cum, cumt, grad, prior, weights),
        WORK, WORK // 100,
        [pltpu.VMEM(*tokens), pltpu.VMEM(*square), pltpu.VMEM(*tokens32), pltpu.SemaphoreType.DMA],
        far_out=(0,),
    )
    grad_k, grad_v, grad_decay, grad_gain = local_call(
        functools.partial(key_gradient_kernel, heads),
        [tokens, tokens, ((heads, length), F32), ((1, width), F32)],
        (key_rows, value_rows, cum, attn, grad, gk_part, gv_part, mine, swap(theirs)),
        WORK, WORK // 100,
        [pltpu.VMEM(*pair_state)],
    )
    return attended, grad_q, grad_k, grad_v, grad_gate, grad_decay.T, grad_gain.reshape(width)


def solution(mesh):
    fine = Mesh(mesh.devices.reshape(4, 8, 2, 4), ("x", "z", "core", "head"))
    tokens = P(("x", "z", "core"), "head")
    return jax.shard_map(
        per_device,
        mesh=fine,
        in_specs=(tokens, tokens, tokens, tokens, P("head"), tokens, tokens),
        out_specs=(tokens, tokens, tokens, tokens, tokens, tokens, P("head")),
        check_vma=False,
    )
```
